32 devices in a mesh: grp: 2 (over x), row: 4 (over y, core), col: 4 (over z).
Axes of the slice: x: 2, y: 2, z: 4, core: 2. Of those that a mesh axis runs over, the one named last changes fastest.
Arguments:
- phase: bfloat16 [64, 2, 128, 2048], P('grp', None, 'row', 'col'), may hold values from -6 to 6
- pseudo_inverse: bfloat16 [48, 64], replicated, may hold values from -0.75 to 0.75
- rotation: float32 [4, 3], replicated, may hold values from -4 to 4
- plate_id: int32 [256, 2048], P(('grp', 'row'), 'col'), may hold values from 0 to 3
- coherent: int32 [256, 2048], P(('grp', 'row'), 'col'), may hold values 0 or 1
Outputs:
- displacement: bfloat16 [48, 256, 2048], P(None, ('grp', 'row'), 'col')
- grad_rows: float32 [256, 2048], P(('grp', 'row'), 'col')
- grad_cols: float32 [256, 2048], P(('grp', 'row'), 'col')
The draws below stay inside these ranges and needn't reach their ends.
All inputs are finite; a program needn't handle non-finite values. No bound on the sum of `coherent` on one device may be relied on, other than what follows from the above.
Results may differ from the reference program's by a relative error of at most 0.001.
Values may be sent and summed in bfloat16 or wider, within the bound.
A program may use at most 128 MiB of HBM per device.

```python
import jax
import jax.numpy as jnp
from jax import lax

IFG = 64
EPOCHS = 48
PLATES = 4
HALF = 16
CY = 32
NY = 256
NX = 2048
BAND = 128
N_GRP = 2
N_ROW = 4


def with_ends(entries, own_key, least, top_value):
    dims = entries.shape
    spot = [jax.random.randint(jax.random.fold_in(own_key, axis), (), 0, dims[axis]) for axis in range(len(dims))]
    entries = entries.at[tuple(spot)].set(least)
    longest = dims.index(max(dims))
    spot[longest] = (spot[longest] + 1) % dims[longest]
    return entries.at[tuple(spot)].set(top_value)


def steps_of(rng, dims, pieces, least, high):
    def one(position, parts):
        heights = jax.random.uniform(jax.random.fold_in(jax.random.fold_in(rng, 6), position), (parts,), jnp.float32, least / len(pieces), high / len(pieces))
        return jnp.repeat(jnp.exp(heights), dims[position] // parts).reshape((-1,) + (1,) * (len(dims) - position - 1))

    factor_of = one(*pieces[0])
    for cut in pieces[1:]:
        factor_of = factor_of * one(*cut)
    return factor_of


def noise(key, dims, deviation, reach, cuts=(), held_as=jnp.bfloat16):
    entries = deviation * jax.random.normal(key, dims, jnp.float32)
    if cuts:
        entries = entries * steps_of(key, dims, cuts, -0.22, 0.18)
    return jnp.clip(entries, -reach, reach).astype(held_as)


def setup_inputs(seed: int = 0) -> dict:
    splits = jax.random.split(jax.random.key(seed), 6)
    phase = noise(splits[0], (IFG, N_GRP, BAND, NX), 1.0, 6.0, ((0, 2), (2, 4), (3, 4)))
    pseudo_inverse = noise(splits[1], (EPOCHS, IFG), IFG ** -0.5, 0.75)
    rotation = noise(splits[2], (PLATES, 3), 1.0, 4.0, (), jnp.float32)
    plate_id = with_ends(jax.random.randint(splits[3], (NY, NX), 0, PLATES), jax.random.fold_in(splits[3], 1), 0, PLATES - 1).astype(jnp.int32)
    coherent = with_ends((jax.random.randint(splits[4], (NY, NX), 0, 4) < 3).astype(jnp.int32), jax.random.fold_in(splits[4], 1), 0, 1)
    return {"phase": phase, "pseudo_inverse": pseudo_inverse, "rotation": rotation, "plate_id": plate_id, "coherent": coherent}


def lever_field(rows, cols):
    lat = jnp.deg2rad(36.0 + 6.0 * (rows + 0.5) / NY)
    lon = jnp.deg2rad(26.0 + 19.0 * (cols + 0.5) / NX)
    px = jnp.cos(lat) * jnp.cos(lon)
    py = jnp.cos(lat) * jnp.sin(lon)
    pz = jnp.sin(lat) + 0.0 * lon
    sx, sy, sz = (0.38, -0.08, 0.92)
    return jnp.stack([py * sz - pz * sy, pz * sx - px * sz, px * sy - py * sx])

def slope_weights():
    steps = jnp.arange(EPOCHS, dtype=jnp.float32) - (EPOCHS - 1) / 2.0
    return steps / jnp.sqrt(jnp.sum(steps * steps))

def reference(phase, pseudo_inverse, rotation, plate_id, coherent):
    bands = N_GRP * N_ROW
    stack = phase.reshape(IFG, bands, CY, NX)
    slope = slope_weights()
    inverse = pseudo_inverse.astype(jnp.float32)

    def one_band(index):
        piece = lax.dynamic_index_in_dim(stack, index, 1, keepdims=False).astype(jnp.float32)
        series = jnp.einsum('ei,iyx->eyx', inverse, piece)
        rate = jnp.einsum('e,eyx->yx', slope, series, precision=lax.Precision.HIGHEST)
        return (series.astype(jnp.bfloat16), rate)
    series_all, rate_all = lax.map(one_band, jnp.arange(bands, dtype=jnp.int32))
    displacement = jnp.transpose(series_all, (1, 0, 2, 3)).reshape(EPOCHS, NY, NX)
    rate = rate_all.reshape(NY, NX)
    rows = jnp.arange(NY, dtype=jnp.float32)[:, None]
    cols = jnp.arange(NX, dtype=jnp.float32)[None, :]
    lever = lever_field(rows, cols)
    plate_rate = jnp.zeros((NY, NX), jnp.float32)
    for plate in range(PLATES):
        along = rotation[plate, 0] * lever[0] + rotation[plate, 1] * lever[1] + rotation[plate, 2] * lever[2]
        plate_rate = plate_rate + jnp.where(plate_id == plate, along, 0.0)
    velocity = coherent.astype(jnp.float32) * rate - plate_rate
    norm = jnp.sqrt(jnp.float32(HALF * (HALF + 1) * (2 * HALF + 1) // 3))
    padded = jnp.pad(velocity, HALF)
    grad_rows = jnp.zeros((NY, NX), jnp.float32)
    grad_cols = jnp.zeros((NY, NX), jnp.float32)
    for k in range(-HALF, HALF + 1):
        tap = k / norm
        grad_rows = grad_rows + tap * padded[HALF + k:HALF + k + NY, HALF:HALF + NX]
        grad_cols = grad_cols + tap * padded[HALF:HALF + NY, HALF + k:HALF + k + NX]
    return (displacement, grad_rows, grad_cols)
```

```python
import functools

import jax
import jax.numpy as jnp
from jax import lax
from jax.experimental import pallas as pl
from jax.experimental.pallas import tpu as pltpu
from jax.sharding import PartitionSpec as P

MESH = pl.DeviceIdType.MESH
REACH = 16
SUB = 16
SPLITS = 3
EARLY, MIDDLE = 2, 3


def iota(shape, dim):
    return lax.broadcasted_iota(jnp.int32, shape, dim)


def parts_of(value):
    high = value.astype(jnp.bfloat16)
    rest = value - high.astype(jnp.float32)
    middle = rest.astype(jnp.bfloat16)
    low = (rest - middle.astype(jnp.float32)).astype(jnp.bfloat16)
    return high, middle, low


def dot(a, b):
    return jnp.dot(a, b, preferred_element_type=jnp.float32)


def as_bf16(mask):
    return jnp.where(mask, 1.0, 0.0).astype(jnp.bfloat16)


def kernel(
    sizes, phase, inverse_hbm, rotation, plate_hbm, coherent_hbm,
    disp, grad_rows, grad_cols,
    stack, mine, inverse, plate, coherent, weights, partial, incoming, tall, wide,
    local_sem, bulk_send, bulk_recv, rate_send, rate_recv, halo_send, halo_recv,
):
    n_grp, n_row, n_col = sizes
    _, share, tile_rows, tile_cols = stack.shape
    epochs, ifgs = inverse.shape
    grp, row, col = lax.axis_index("grp"), lax.axis_index("row"), lax.axis_index("col")
    tile = grp * n_row + row
    tiles = n_grp * n_row

    locals_ = [
        pltpu.make_async_copy(inverse_hbm, inverse, local_sem.at[0]),
        pltpu.make_async_copy(plate_hbm, plate, local_sem.at[1]),
        pltpu.make_async_copy(coherent_hbm, coherent, local_sem.at[2]),
        pltpu.make_async_copy(phase.at[:, grp], stack.at[0], local_sem.at[3]),
    ]
    targets = [lax.rem(grp + s, n_grp) for s in range(n_grp)]
    for s in range(1, n_grp):
        locals_.append(
            pltpu.make_async_copy(phase.at[:, targets[s]], mine.at[s - 1], local_sem.at[3 + s])
        )
    for copy in locals_:
        copy.start()

    above, below = tile - 1, tile + 1
    places = [
        {"grp": lax.div(jnp.maximum(above, 0), n_row), "row": lax.rem(jnp.maximum(above, 0), n_row)},
        {"grp": lax.rem(lax.div(below, n_row), n_grp), "row": lax.rem(below, n_row)},
        {"col": jnp.maximum(col - 1, 0)},
        {"col": jnp.minimum(col + 1, n_col - 1)},
    ]
    there = [tile > 0, tile < tiles - 1, col > 0, col < n_col - 1]

    barrier = pltpu.get_barrier_semaphore()
    for s in range(1, n_grp):
        pl.semaphore_signal(barrier, inc=1, device_id={"grp": targets[s]}, device_id_type=MESH)
    for place, exists in zip(places, there):
        @pl.when(exists)
        def _(place=place):
            pl.semaphore_signal(barrier, inc=1, device_id=place, device_id_type=MESH)
    peers = n_grp - 1
    for exists in there:
        peers = peers + jnp.where(exists, 1, 0)
    pl.semaphore_wait(barrier, peers)

    half = tile_cols // 2
    chunks = [(y, x) for y in range(0, tile_rows, SUB) for x in range(0, tile_cols, half)]

    def bulk(s, c):
        y, x = chunks[c]
        return pltpu.make_async_remote_copy(
            src_ref=phase.at[:, targets[s], pl.ds(y, SUB), pl.ds(x, half)],
            dst_ref=stack.at[s, :, pl.ds(y, SUB), pl.ds(x, half)],
            send_sem=bulk_send.at[s - 1, c],
            recv_sem=bulk_recv.at[s - 1, c],
            device_id={"grp": targets[s]},
            device_id_type=MESH,
        )

    bulks = [[bulk(s, c) for s in range(1, n_grp)] for c in range(len(chunks))]
    for c in range(EARLY):
        for copy in bulks[c]:
            copy.start()

    locals_[0].wait()
    steps = iota((epochs, 1), 0).astype(jnp.float32) - (epochs - 1) / 2.0
    slope = steps / jnp.sqrt(jnp.sum(steps * steps, axis=0, keepdims=True))
    rate_weight = jnp.sum(inverse[...].astype(jnp.float32) * slope, axis=0, keepdims=True)
    high, middle, low = parts_of(rate_weight)
    pick = iota((SPLITS * SUB, ifgs), 0) // SUB
    spread = jnp.where(
        pick == 0,
        high.astype(jnp.float32),
        jnp.where(pick == 1, middle.astype(jnp.float32), low.astype(jnp.float32)),
    ).astype(jnp.bfloat16)
    depth = share * SUB
    own = as_bf16(iota((ifgs, depth), 0) == grp * share + iota((ifgs, depth), 1) // SUB)
    diagonal = (iota((SPLITS * SUB, depth), 0) & (SUB - 1)) == (
        iota((SPLITS * SUB, depth), 1) & (SUB - 1)
    )
    rate_matrix = jnp.where(diagonal, dot(spread, own), 0.0).astype(jnp.bfloat16)

    def partial_rate(block, slot):
        for y in range(0, tile_rows, SUB):
            data = block[:, pl.ds(y, SUB), :].reshape(depth, tile_cols)
            three = dot(rate_matrix, data)
            partial[slot, pl.ds(y, SUB), :] = (
                three[:SUB] + three[SUB:2 * SUB] + three[2 * SUB:]
            )

    rates = []
    for s in range(1, n_grp):
        locals_[3 + s].wait()
        partial_rate(mine.at[s - 1], s)
        rates.append(
            pltpu.make_async_remote_copy(
                src_ref=partial.at[s],
                dst_ref=incoming.at[s - 1],
                send_sem=rate_send.at[s - 1],
                recv_sem=rate_recv.at[s - 1],
                device_id={"grp": targets[s]},
                device_id_type=MESH,
            )
        )
        rates[-1].start()
    for c in range(EARLY, MIDDLE):
        for copy in bulks[c]:
            copy.start()
    locals_[3].wait()
    partial_rate(stack.at[0], 0)

    locals_[1].wait()
    locals_[2].wait()
    ys = (tile * tile_rows + iota((tile_rows, 128), 0)).astype(jnp.float32)
    xs = (col * tile_cols + iota((8, tile_cols), 1)).astype(jnp.float32)
    lat = jnp.deg2rad(36.0 + 6.0 * (ys + 0.5) / (tiles * tile_rows))
    lon = jnp.deg2rad(26.0 + 19.0 * (xs + 0.5) / (n_col * tile_cols))
    cos_lat, sin_lat = jnp.cos(lat)[:, :1], jnp.sin(lat)[:, :1]
    cos_lon, sin_lon = jnp.cos(lon)[:1], jnp.sin(lon)[:1]
    px, py = cos_lat * cos_lon, cos_lat * sin_lon
    pz = sin_lat + jnp.zeros_like(px)
    sx, sy, sz = (0.38, -0.08, 0.92)
    lever = (py * sz - pz * sy, pz * sx - px * sz, px * sy - py * sx)
    plate_rate = jnp.zeros((tile_rows, tile_cols), jnp.float32)
    for p in range(rotation.shape[0]):
        along = rotation[p, 0] * lever[0] + rotation[p, 1] * lever[1] + rotation[p, 2] * lever[2]
        plate_rate = jnp.where(plate[...] == p, along, plate_rate)

    rate = partial[0]
    for s in range(1, n_grp):
        rates[s - 1].wait_recv()
        rate = rate + incoming[s - 1]
    velocity = coherent[...].astype(jnp.float32) * rate - plate_rate
    tall[pl.ds(REACH, tile_rows), :] = velocity
    wide[:, pl.ds(128, tile_cols)] = velocity

    halo_from = [
        tall.at[pl.ds(REACH, REACH), :],
        tall.at[pl.ds(tile_rows, REACH), :],
        wide.at[:, pl.ds(128, 128)],
        wide.at[:, pl.ds(tile_cols, 128)],
    ]
    halo_to = [
        tall.at[pl.ds(REACH + tile_rows, REACH), :],
        tall.at[pl.ds(0, REACH), :],
        wide.at[:, pl.ds(128 + tile_cols, 128)],
        wide.at[:, pl.ds(0, 128)],
    ]
    opposite = [1, 0, 3, 2]
    halos = [
        pltpu.make_async_remote_copy(
            src_ref=halo_from[d],
            dst_ref=halo_to[d],
            send_sem=halo_send.at[d],
            recv_sem=halo_recv.at[d],
            device_id=places[d],
            device_id_type=MESH,
        )
        for d in range(4)
    ]
    for d in range(4):
        pl.when(there[d])(halos[d].start)
    for c in range(MIDDLE, len(chunks)):
        for copy in bulks[c]:
            copy.start()

    full = ifgs * SUB
    rows_of = as_bf16(iota((epochs * SUB, epochs), 0) // SUB == iota((epochs * SUB, epochs), 1))
    tall_inverse = dot(rows_of, inverse[...]).astype(jnp.bfloat16)
    for s in range(n_grp):
        source = lax.rem(grp + n_grp - s, n_grp)
        spot = as_bf16(iota((ifgs, depth), 0) == source * share + iota((ifgs, depth), 1) // SUB)
        same = (iota((epochs * SUB, depth), 0) & (SUB - 1)) == (
            iota((epochs * SUB, depth), 1) & (SUB - 1)
        )
        weights[:, pl.ds(s * depth, depth)] = jnp.where(same, dot(tall_inverse, spot), 0.0).astype(
            jnp.bfloat16
        )

    def series(c):
        y, x = chunks[c]
        for copy in bulks[c]:
            copy.wait_recv()
        data = stack[:, :, pl.ds(y, SUB), pl.ds(x, half)].reshape(full, half)
        out = dot(weights[...], data).reshape(epochs, SUB, half)
        disp[:, pl.ds(y, SUB), pl.ds(x, half)] = out.astype(jnp.bfloat16)

    for c in range(EARLY):
        series(c)

    for d in range(4):
        pl.when(there[d])(halos[d].wait_send)
        pl.when(there[opposite[d]])(halos[d].wait_recv)

        @pl.when(jnp.logical_not(there[opposite[d]]))
        def _(d=d):
            halo_to[d][...] = jnp.zeros(halo_to[d].shape, jnp.float32)
    scale = 1.0 / (float(REACH * (REACH + 1) * (2 * REACH + 1) // 3) ** 0.5)
    shape = (tile_rows, tile_rows + 2 * REACH)
    k = iota(shape, 1) - REACH - iota(shape, 0)
    taps = jnp.where(jnp.abs(k) <= REACH, k, 0).astype(jnp.float32).astype(jnp.bfloat16)
    total = None
    for part in parts_of(tall[...]):
        term = dot(taps, part)
        total = term if total is None else total + term
    grad_rows[...] = total * scale
    shape = (tile_cols + 256, tile_cols)
    k = iota(shape, 0) - 128 - iota(shape, 1)
    taps = jnp.where(jnp.abs(k) <= REACH, k, 0).astype(jnp.float32).astype(jnp.bfloat16)
    total = None
    for part in parts_of(wide[...]):
        term = dot(part, taps)
        total = term if total is None else total + term
    grad_cols[...] = total * scale

    for c in range(EARLY, len(chunks)):
        series(c)
    for c in range(len(chunks)):
        for copy in bulks[c]:
            copy.wait_send()
    for copy in rates:
        copy.wait_send()


def on_device(sizes, phase, pseudo_inverse, rotation, plate_id, coherent):
    share, n_grp, tile_rows, tile_cols = phase.shape
    epochs, ifgs = pseudo_inverse.shape
    anywhere = pl.BlockSpec(memory_space=pl.ANY)
    vmem = pl.BlockSpec(memory_space=pltpu.VMEM)
    f32, bf16 = jnp.float32, jnp.bfloat16
    others = n_grp - 1
    chunks = (tile_rows // SUB) * 2
    dma = pltpu.SemaphoreType.DMA
    return pl.pallas_call(
        functools.partial(kernel, sizes),
        out_shape=(
            jax.ShapeDtypeStruct((epochs, tile_rows, tile_cols), bf16),
            jax.ShapeDtypeStruct((tile_rows, tile_cols), f32),
            jax.ShapeDtypeStruct((tile_rows, tile_cols), f32),
        ),
        in_specs=[
            anywhere, anywhere, pl.BlockSpec(memory_space=pltpu.SMEM), anywhere, anywhere,
        ],
        out_specs=(vmem, vmem, vmem),
        scratch_shapes=[
            pltpu.VMEM((n_grp, share, tile_rows, tile_cols), bf16),
            pltpu.VMEM((others, share, tile_rows, tile_cols), bf16),
            pltpu.VMEM((epochs, ifgs), bf16),
            pltpu.VMEM((tile_rows, tile_cols), jnp.int32),
            pltpu.VMEM((tile_rows, tile_cols), jnp.int32),
            pltpu.VMEM((epochs * SUB, ifgs * SUB), bf16),
            pltpu.VMEM((n_grp, tile_rows, tile_cols), f32),
            pltpu.VMEM((others, tile_rows, tile_cols), f32),
            pltpu.VMEM((tile_rows + 2 * REACH, tile_cols), f32),
            pltpu.VMEM((tile_rows, tile_cols + 256), f32),
            dma((3 + n_grp,)),
            dma((others, chunks)),
            dma((others, chunks)),
            dma((others,)),
            dma((others,)),
            dma((4,)),
            dma((4,)),
        ],
        compiler_params=pltpu.CompilerParams(
            collective_id=0, has_side_effects=True, vmem_limit_bytes=48 * 1024 * 1024
        ),
        cost_estimate=pl.CostEstimate(
            flops=2 * epochs * ifgs * SUB * tile_rows * tile_cols,
            bytes_accessed=8 * 1024 * 1024,
            transcendentals=0,
        ),
    )(phase, pseudo_inverse, rotation, plate_id, coherent)


def solution(mesh):
    sizes = (mesh.shape["grp"], mesh.shape["row"], mesh.shape["col"])
    return jax.shard_map(
        functools.partial(on_device, sizes),
        mesh=mesh,
        in_specs=(
            P("grp", None, "row", "col"),
            P(),
            P(),
            P(("grp", "row"), "col"),
            P(("grp", "row"), "col"),
        ),
        out_specs=(
            P(None, ("grp", "row"), "col"),
            P(("grp", "row"), "col"),
            P(("grp", "row"), "col"),
        ),
        check_vma=False,
    )
```

```python
import functools

import jax
import jax.numpy as jnp
from jax import lax
from jax.experimental import pallas as pl
from jax.experimental.pallas import tpu as pltpu
from jax.sharding import PartitionSpec as P

MESH = pl.DeviceIdType.MESH
REACH = 16
SUB = 16
SPLITS = 3
GRANT = 63 * 1024 * 1024
PIECES = 8
EARLY, MIDDLE = 2, 3


def iota(shape, dim):
    return lax.broadcasted_iota(jnp.int32, shape, dim)


def parts_of(value):
    high = value.astype(jnp.bfloat16)
    rest = value - high.astype(jnp.float32)
    middle = rest.astype(jnp.bfloat16)
    low = (rest - middle.astype(jnp.float32)).astype(jnp.bfloat16)
    return high, middle, low


def dot(a, b):
    return jnp.dot(a, b, preferred_element_type=jnp.float32)


def as_bf16(mask):
    return jnp.where(mask, 1.0, 0.0).astype(jnp.bfloat16)


def kernel(
    sizes, phase, inverse_hbm, rotation_hbm, plate_hbm, coherent_hbm,
    disp_hbm, grad_rows_hbm, grad_cols_hbm,
    disp, grad_rows, grad_cols, stack, mine, inverse, rotation, plate, coherent, weights, partial, incoming, tall, wide,
    local_sem, bulk_send, bulk_recv, rate_send, rate_recv, halo_send, halo_recv, out_sem,
):
    n_grp, n_row, n_col = sizes
    _, share, tile_rows, tile_cols = stack.shape
    epochs, ifgs = inverse.shape
    grp, row, col = lax.axis_index("grp"), lax.axis_index("row"), lax.axis_index("col")
    tile = grp * n_row + row
    tiles = n_grp * n_row

    locals_ = [
        pltpu.make_async_copy(inverse_hbm, inverse, local_sem.at[0]),
        pltpu.make_async_copy(plate_hbm, plate, local_sem.at[1]),
        pltpu.make_async_copy(coherent_hbm, coherent, local_sem.at[2]),
        pltpu.make_async_copy(phase.at[:, grp], stack.at[0], local_sem.at[3]),
        pltpu.make_async_copy(rotation_hbm, rotation, local_sem.at[4]),
    ]
    targets = [lax.rem(grp + s, n_grp) for s in range(n_grp)]
    for s in range(1, n_grp):
        locals_.append(
            pltpu.make_async_copy(phase.at[:, targets[s]], mine.at[s - 1], local_sem.at[4 + s])
        )
    for copy in locals_:
        copy.start()

    above, below = tile - 1, tile + 1
    places = [
        {"grp": lax.div(jnp.maximum(above, 0), n_row), "row": lax.rem(jnp.maximum(above, 0), n_row)},
        {"grp": lax.rem(lax.div(below, n_row), n_grp), "row": lax.rem(below, n_row)},
        {"col": jnp.maximum(col - 1, 0)},
        {"col": jnp.minimum(col + 1, n_col - 1)},
    ]
    there = [tile > 0, tile < tiles - 1, col > 0, col < n_col - 1]

    barrier = pltpu.get_barrier_semaphore()
    for s in range(1, n_grp):
        pl.semaphore_signal(barrier, inc=1, device_id={"grp": targets[s]}, device_id_type=MESH)
    for place, exists in zip(places, there):
        @pl.when(exists)
        def _(place=place):
            pl.semaphore_signal(barrier, inc=1, device_id=place, device_id_type=MESH)
    peers = n_grp - 1
    for exists in there:
        peers = peers + jnp.where(exists, 1, 0)
    pl.semaphore_wait(barrier, peers)

    half = tile_cols // 2
    chunks = [(y, x) for y in range(0, tile_rows, SUB) for x in range(0, tile_cols, half)]

    def bulk(s, c):
        y, x = chunks[c]
        return pltpu.make_async_remote_copy(
            src_ref=phase.at[:, targets[s], pl.ds(y, SUB), pl.ds(x, half)],
            dst_ref=stack.at[s, :, pl.ds(y, SUB), pl.ds(x, half)],
            send_sem=bulk_send.at[s - 1, c],
            recv_sem=bulk_recv.at[s - 1, c],
            device_id={"grp": targets[s]},
            device_id_type=MESH,
        )

    bulks = [[bulk(s, c) for s in range(1, n_grp)] for c in range(len(chunks))]
    for c in range(EARLY):
        for copy in bulks[c]:
            copy.start()

    locals_[0].wait()
    steps = iota((epochs, 1), 0).astype(jnp.float32) - (epochs - 1) / 2.0
    slope = steps / jnp.sqrt(jnp.sum(steps * steps, axis=0, keepdims=True))
    rate_weight = jnp.sum(inverse[...].astype(jnp.float32) * slope, axis=0, keepdims=True)
    high, middle, low = parts_of(rate_weight)
    pick = iota((SPLITS * SUB, ifgs), 0) // SUB
    spread = jnp.where(
        pick == 0,
        high.astype(jnp.float32),
        jnp.where(pick == 1, middle.astype(jnp.float32), low.astype(jnp.float32)),
    ).astype(jnp.bfloat16)
    depth = share * SUB
    own = as_bf16(iota((ifgs, depth), 0) == grp * share + iota((ifgs, depth), 1) // SUB)
    diagonal = (iota((SPLITS * SUB, depth), 0) & (SUB - 1)) == (
        iota((SPLITS * SUB, depth), 1) & (SUB - 1)
    )
    rate_matrix = jnp.where(diagonal, dot(spread, own), 0.0).astype(jnp.bfloat16)

    def partial_rate(block, slot):
        for y in range(0, tile_rows, SUB):
            data = block[:, pl.ds(y, SUB), :].reshape(depth, tile_cols)
            three = dot(rate_matrix, data)
            partial[slot, pl.ds(y, SUB), :] = (
                three[:SUB] + three[SUB:2 * SUB] + three[2 * SUB:]
            )

    rates = []
    for s in range(1, n_grp):
        locals_[4 + s].wait()
        partial_rate(mine.at[s - 1], s)
        rates.append(
            pltpu.make_async_remote_copy(
                src_ref=partial.at[s],
                dst_ref=incoming.at[s - 1],
                send_sem=rate_send.at[s - 1],
                recv_sem=rate_recv.at[s - 1],
                device_id={"grp": targets[s]},
                device_id_type=MESH,
            )
        )
        rates[-1].start()
    for c in range(EARLY, MIDDLE):
        for copy in bulks[c]:
            copy.start()
    locals_[3].wait()
    partial_rate(stack.at[0], 0)

    locals_[1].wait()
    locals_[2].wait()
    locals_[4].wait()
    ys = (tile * tile_rows + iota((tile_rows, 128), 0)).astype(jnp.float32)
    xs = (col * tile_cols + iota((8, tile_cols), 1)).astype(jnp.float32)
    lat = jnp.deg2rad(36.0 + 6.0 * (ys + 0.5) / (tiles * tile_rows))
    lon = jnp.deg2rad(26.0 + 19.0 * (xs + 0.5) / (n_col * tile_cols))
    cos_lat, sin_lat = jnp.cos(lat)[:, :1], jnp.sin(lat)[:, :1]
    cos_lon, sin_lon = jnp.cos(lon)[:1], jnp.sin(lon)[:1]
    px, py = cos_lat * cos_lon, cos_lat * sin_lon
    pz = sin_lat + jnp.zeros_like(px)
    sx, sy, sz = (0.38, -0.08, 0.92)
    lever = (py * sz - pz * sy, pz * sx - px * sz, px * sy - py * sx)
    plate_rate = jnp.zeros((tile_rows, tile_cols), jnp.float32)
    for p in range(rotation.shape[0]):
        along = rotation[p, 0] * lever[0] + rotation[p, 1] * lever[1] + rotation[p, 2] * lever[2]
        plate_rate = jnp.where(plate[...] == p, along, plate_rate)

    rate = partial[0]
    for s in range(1, n_grp):
        rates[s - 1].wait_recv()
        rate = rate + incoming[s - 1]
    velocity = coherent[...].astype(jnp.float32) * rate - plate_rate
    tall[pl.ds(REACH, tile_rows), :] = velocity
    wide[:, pl.ds(128, tile_cols)] = velocity

    halo_from = [
        tall.at[pl.ds(REACH, REACH), :],
        tall.at[pl.ds(tile_rows, REACH), :],
        wide.at[:, pl.ds(128, 128)],
        wide.at[:, pl.ds(tile_cols, 128)],
    ]
    halo_to = [
        tall.at[pl.ds(REACH + tile_rows, REACH), :],
        tall.at[pl.ds(0, REACH), :],
        wide.at[:, pl.ds(128 + tile_cols, 128)],
        wide.at[:, pl.ds(0, 128)],
    ]
    opposite = [1, 0, 3, 2]
    halos = [
        pltpu.make_async_remote_copy(
            src_ref=halo_from[d],
            dst_ref=halo_to[d],
            send_sem=halo_send.at[d],
            recv_sem=halo_recv.at[d],
            device_id=places[d],
            device_id_type=MESH,
        )
        for d in range(4)
    ]
    for d in range(4):
        pl.when(there[d])(halos[d].start)
    for c in range(MIDDLE, len(chunks)):
        for copy in bulks[c]:
            copy.start()

    full = ifgs * SUB
    rows_of = as_bf16(iota((epochs * SUB, epochs), 0) // SUB == iota((epochs * SUB, epochs), 1))
    tall_inverse = dot(rows_of, inverse[...]).astype(jnp.bfloat16)
    for s in range(n_grp):
        source = lax.rem(grp + n_grp - s, n_grp)
        spot = as_bf16(iota((ifgs, depth), 0) == source * share + iota((ifgs, depth), 1) // SUB)
        same = (iota((epochs * SUB, depth), 0) & (SUB - 1)) == (
            iota((epochs * SUB, depth), 1) & (SUB - 1)
        )
        weights[:, pl.ds(s * depth, depth)] = jnp.where(same, dot(tall_inverse, spot), 0.0).astype(
            jnp.bfloat16
        )

    def series(c):
        y, x = chunks[c]
        for copy in bulks[c]:
            copy.wait_recv()
        data = stack[:, :, pl.ds(y, SUB), pl.ds(x, half)].reshape(full, half)
        out = dot(weights[...], data).reshape(epochs, SUB, half)
        disp[:, pl.ds(y, SUB), pl.ds(x, half)] = out.astype(jnp.bfloat16)
        write(
            disp.at[:, pl.ds(y, SUB), pl.ds(x, half)],
            disp_hbm.at[:, pl.ds(y, SUB), pl.ds(x, half)],
        )

    writes = []

    def write(source, target):
        writes.append(pltpu.make_async_copy(source, target, out_sem.at[len(writes)]))
        writes[-1].start()

    for c in range(EARLY):
        series(c)

    for d in range(4):
        pl.when(there[d])(halos[d].wait_send)
        pl.when(there[opposite[d]])(halos[d].wait_recv)

        @pl.when(jnp.logical_not(there[opposite[d]]))
        def _(d=d):
            halo_to[d][...] = jnp.zeros(halo_to[d].shape, jnp.float32)
    scale = 1.0 / (float(REACH * (REACH + 1) * (2 * REACH + 1) // 3) ** 0.5)
    shape = (tile_rows, tile_rows + 2 * REACH)
    k = iota(shape, 1) - REACH - iota(shape, 0)
    taps = jnp.where(jnp.abs(k) <= REACH, k, 0).astype(jnp.float32).astype(jnp.bfloat16)
    total = None
    for part in parts_of(tall[...]):
        term = dot(taps, part)
        total = term if total is None else total + term
    grad_rows[...] = total * scale
    shape = (tile_cols + 256, tile_cols)
    k = iota(shape, 0) - 128 - iota(shape, 1)
    taps = jnp.where(jnp.abs(k) <= REACH, k, 0).astype(jnp.float32).astype(jnp.bfloat16)
    total = None
    for part in parts_of(wide[...]):
        term = dot(part, taps)
        total = term if total is None else total + term
    grad_cols[...] = total * scale
    write(grad_rows, grad_rows_hbm)
    write(grad_cols, grad_cols_hbm)

    for c in range(EARLY, len(chunks)):
        series(c)
    for c in range(len(chunks)):
        for copy in bulks[c]:
            copy.wait_send()
    for copy in rates:
        copy.wait_send()
    for copy in writes:
        copy.wait()


def write_out(disp, grad_rows, grad_cols, disp_hbm, grad_rows_hbm, grad_cols_hbm, sem):
    copies = [
        pltpu.make_async_copy(grad_rows, grad_rows_hbm, sem.at[0]),
        pltpu.make_async_copy(grad_cols, grad_cols_hbm, sem.at[1]),
    ]
    size = disp.shape[0] // PIECES
    for i in range(PIECES):
        rows = pl.ds(i * size, size)
        copies.append(pltpu.make_async_copy(disp.at[rows], disp_hbm.at[rows], sem.at[2 + i]))
    for copy in copies:
        copy.start()
    for copy in copies:
        copy.wait()


def on_device(sizes, phase, pseudo_inverse, rotation, plate_id, coherent):
    share, n_grp, tile_rows, tile_cols = phase.shape
    epochs, ifgs = pseudo_inverse.shape
    hbm = pl.BlockSpec(memory_space=pltpu.HBM)
    f32, bf16 = jnp.float32, jnp.bfloat16
    others = n_grp - 1
    chunks = (tile_rows // SUB) * 2
    dma = pltpu.SemaphoreType.DMA
    results = pl.pallas_call(
        functools.partial(kernel, sizes),
        out_shape=(
            jax.ShapeDtypeStruct((epochs, tile_rows, tile_cols), bf16),
            jax.ShapeDtypeStruct((tile_rows, tile_cols), f32),
            jax.ShapeDtypeStruct((tile_rows, tile_cols), f32),
        ),
        in_specs=[
            hbm, hbm, hbm, hbm, hbm,
        ],
        out_specs=(hbm, hbm, hbm),
        scratch_shapes=[
            pltpu.VMEM((epochs, tile_rows, tile_cols), bf16),
            pltpu.VMEM((tile_rows, tile_cols), f32),
            pltpu.VMEM((tile_rows, tile_cols), f32),
            pltpu.VMEM((n_grp, share, tile_rows, tile_cols), bf16),
            pltpu.VMEM((others, share, tile_rows, tile_cols), bf16),
            pltpu.VMEM((epochs, ifgs), bf16),
            pltpu.SMEM(rotation.shape, f32),
            pltpu.VMEM((tile_rows, tile_cols), jnp.int32),
            pltpu.VMEM((tile_rows, tile_cols), jnp.int32),
            pltpu.VMEM((epochs * SUB, ifgs * SUB), bf16),
            pltpu.VMEM((n_grp, tile_rows, tile_cols), f32),
            pltpu.VMEM((others, tile_rows, tile_cols), f32),
            pltpu.VMEM((tile_rows + 2 * REACH, tile_cols), f32),
            pltpu.VMEM((tile_rows, tile_cols + 256), f32),
            dma((4 + n_grp,)),
            dma((others, chunks)),
            dma((others, chunks)),
            dma((others,)),
            dma((others,)),
            dma((4,)),
            dma((4,)),
            dma((chunks + 2,)),
        ],
        compiler_params=pltpu.CompilerParams(
            collective_id=0, has_side_effects=True, vmem_limit_bytes=GRANT
        ),
        cost_estimate=pl.CostEstimate(
            flops=2 * epochs * ifgs * SUB * tile_rows * tile_cols,
            bytes_accessed=8 * 1024 * 1024,
            transcendentals=0,
        ),
    )(phase, pseudo_inverse, rotation, plate_id, coherent)
    return pl.pallas_call(
        write_out,
        out_shape=tuple(jax.ShapeDtypeStruct(r.shape, r.dtype) for r in results),
        in_specs=[hbm] * 3,
        out_specs=(hbm,) * 3,
        scratch_shapes=[dma((2 + PIECES,))],
        compiler_params=pltpu.CompilerParams(vmem_limit_bytes=GRANT),
    )(*results)


def solution(mesh):
    sizes = (mesh.shape["grp"], mesh.shape["row"], mesh.shape["col"])
    return jax.shard_map(
        functools.partial(on_device, sizes),
        mesh=mesh,
        in_specs=(
            P("grp", None, "row", "col"),
            P(),
            P(),
            P(("grp", "row"), "col"),
            P(("grp", "row"), "col"),
        ),
        out_specs=(
            P(None, ("grp", "row"), "col"),
            P(("grp", "row"), "col"),
            P(("grp", "row"), "col"),
        ),
        check_vma=False,
    )
```

```python
import functools

import jax
import jax.numpy as jnp
from jax import lax
from jax.experimental import pallas as pl
from jax.experimental.pallas import tpu as pltpu
from jax.sharding import PartitionSpec as P

MESH = pl.DeviceIdType.MESH
REACH = 16
SUB = 16
SPLITS = 3
GRANT = 63 * 1024 * 1024
PIECES = 4
EARLY, MIDDLE = 2, 4


def iota(shape, dim):
    return lax.broadcasted_iota(jnp.int32, shape, dim)


def parts_of(value):
    high = value.astype(jnp.bfloat16)
    rest = value - high.astype(jnp.float32)
    middle = rest.astype(jnp.bfloat16)
    low = (rest - middle.astype(jnp.float32)).astype(jnp.bfloat16)
    return high, middle, low


def dot(a, b):
    return jnp.dot(a, b, preferred_element_type=jnp.float32)


def as_bf16(mask):
    return jnp.where(mask, 1.0, 0.0).astype(jnp.bfloat16)


def kernel(
    sizes, phase, inverse_hbm, rotation_hbm, plate_hbm, coherent_hbm,
    disp_hbm, grad_rows_hbm, grad_cols_hbm,
    disp, grad_rows, grad_cols, stack, mine, inverse, rotation, plate, coherent, weights, partial, incoming, tall, wide,
    local_sem, bulk_send, bulk_recv, rate_send, rate_recv, halo_send, halo_recv, out_sem,
):
    n_grp, n_row, n_col = sizes
    _, share, tile_rows, tile_cols = stack.shape
    epochs, ifgs = inverse.shape
    grp, row, col = lax.axis_index("grp"), lax.axis_index("row"), lax.axis_index("col")
    tile = grp * n_row + row
    tiles = n_grp * n_row

    locals_ = [
        pltpu.make_async_copy(inverse_hbm, inverse, local_sem.at[0]),
        pltpu.make_async_copy(plate_hbm, plate, local_sem.at[1]),
        pltpu.make_async_copy(coherent_hbm, coherent, local_sem.at[2]),
        pltpu.make_async_copy(phase.at[:, grp], stack.at[0], local_sem.at[3]),
        pltpu.make_async_copy(rotation_hbm, rotation, local_sem.at[4]),
    ]
    targets = [lax.rem(grp + s, n_grp) for s in range(n_grp)]
    for s in range(1, n_grp):
        locals_.append(
            pltpu.make_async_copy(phase.at[:, targets[s]], mine.at[s - 1], local_sem.at[4 + s])
        )
    for copy in locals_:
        copy.start()

    above, below = tile - 1, tile + 1
    places = [
        {"grp": lax.div(jnp.maximum(above, 0), n_row), "row": lax.rem(jnp.maximum(above, 0), n_row)},
        {"grp": lax.rem(lax.div(below, n_row), n_grp), "row": lax.rem(below, n_row)},
        {"col": jnp.maximum(col - 1, 0)},
        {"col": jnp.minimum(col + 1, n_col - 1)},
    ]
    there = [tile > 0, tile < tiles - 1, col > 0, col < n_col - 1]

    barrier = pltpu.get_barrier_semaphore()
    for s in range(1, n_grp):
        pl.semaphore_signal(barrier, inc=1, device_id={"grp": targets[s]}, device_id_type=MESH)
    for place, exists in zip(places, there):
        @pl.when(exists)
        def _(place=place):
            pl.semaphore_signal(barrier, inc=1, device_id=place, device_id_type=MESH)
    peers = n_grp - 1
    for exists in there:
        peers = peers + jnp.where(exists, 1, 0)
    pl.semaphore_wait(barrier, peers)

    half = tile_cols // 2
    chunks = [(y, x) for y in range(0, tile_rows, SUB) for x in range(0, tile_cols, half)]

    def bulk(s, c):
        y, x = chunks[c]
        return pltpu.make_async_remote_copy(
            src_ref=phase.at[:, targets[s], pl.ds(y, SUB), pl.ds(x, half)],
            dst_ref=stack.at[s, :, pl.ds(y, SUB), pl.ds(x, half)],
            send_sem=bulk_send.at[s - 1, c],
            recv_sem=bulk_recv.at[s - 1, c],
            device_id={"grp": targets[s]},
            device_id_type=MESH,
        )

    bulks = [[bulk(s, c) for s in range(1, n_grp)] for c in range(len(chunks))]
    for c in range(EARLY):
        for copy in bulks[c]:
            copy.start()

    locals_[0].wait()
    steps = iota((epochs, 1), 0).astype(jnp.float32) - (epochs - 1) / 2.0
    slope = steps / jnp.sqrt(jnp.sum(steps * steps, axis=0, keepdims=True))
    rate_weight = jnp.sum(inverse[...].astype(jnp.float32) * slope, axis=0, keepdims=True)
    high, middle, low = parts_of(rate_weight)
    pick = iota((SPLITS * SUB, ifgs), 0) // SUB
    spread = jnp.where(
        pick == 0,
        high.astype(jnp.float32),
        jnp.where(pick == 1, middle.astype(jnp.float32), low.astype(jnp.float32)),
    ).astype(jnp.bfloat16)
    depth = share * SUB
    own = as_bf16(iota((ifgs, depth), 0) == grp * share + iota((ifgs, depth), 1) // SUB)
    diagonal = (iota((SPLITS * SUB, depth), 0) & (SUB - 1)) == (
        iota((SPLITS * SUB, depth), 1) & (SUB - 1)
    )
    rate_matrix = jnp.where(diagonal, dot(spread, own), 0.0).astype(jnp.bfloat16)

    def partial_rate(block, slot):
        for y in range(0, tile_rows, SUB):
            data = block[:, pl.ds(y, SUB), :].reshape(depth, tile_cols)
            three = dot(rate_matrix, data)
            partial[slot, pl.ds(y, SUB), :] = (
                three[:SUB] + three[SUB:2 * SUB] + three[2 * SUB:]
            )

    rates = []
    for s in range(1, n_grp):
        locals_[4 + s].wait()
        partial_rate(mine.at[s - 1], s)
        rates.append(
            pltpu.make_async_remote_copy(
                src_ref=partial.at[s],
                dst_ref=incoming.at[s - 1],
                send_sem=rate_send.at[s - 1],
                recv_sem=rate_recv.at[s - 1],
                device_id={"grp": targets[s]},
                device_id_type=MESH,
            )
        )
        rates[-1].start()
    for c in range(EARLY, MIDDLE):
        for copy in bulks[c]:
            copy.start()
    locals_[3].wait()
    partial_rate(stack.at[0], 0)

    locals_[1].wait()
    locals_[2].wait()
    locals_[4].wait()
    ys = (tile * tile_rows + iota((tile_rows, 128), 0)).astype(jnp.float32)
    xs = (col * tile_cols + iota((8, tile_cols), 1)).astype(jnp.float32)
    lat = jnp.deg2rad(36.0 + 6.0 * (ys + 0.5) / (tiles * tile_rows))
    lon = jnp.deg2rad(26.0 + 19.0 * (xs + 0.5) / (n_col * tile_cols))
    cos_lat, sin_lat = jnp.cos(lat)[:, :1], jnp.sin(lat)[:, :1]
    cos_lon, sin_lon = jnp.cos(lon)[:1], jnp.sin(lon)[:1]
    px, py = cos_lat * cos_lon, cos_lat * sin_lon
    pz = sin_lat + jnp.zeros_like(px)
    sx, sy, sz = (0.38, -0.08, 0.92)
    lever = (py * sz - pz * sy, pz * sx - px * sz, px * sy - py * sx)
    plate_rate = jnp.zeros((tile_rows, tile_cols), jnp.float32)
    for p in range(rotation.shape[0]):
        along = rotation[p, 0] * lever[0] + rotation[p, 1] * lever[1] + rotation[p, 2] * lever[2]
        plate_rate = jnp.where(plate[...] == p, along, plate_rate)

    rate = partial[0]
    for s in range(1, n_grp):
        rates[s - 1].wait_recv()
        rate = rate + incoming[s - 1]
    velocity = coherent[...].astype(jnp.float32) * rate - plate_rate
    tall[pl.ds(REACH, tile_rows), :] = velocity
    wide[:, pl.ds(128, tile_cols)] = velocity

    halo_from = [
        tall.at[pl.ds(REACH, REACH), :],
        tall.at[pl.ds(tile_rows, REACH), :],
        wide.at[:, pl.ds(128, 128)],
        wide.at[:, pl.ds(tile_cols, 128)],
    ]
    halo_to = [
        tall.at[pl.ds(REACH + tile_rows, REACH), :],
        tall.at[pl.ds(0, REACH), :],
        wide.at[:, pl.ds(128 + tile_cols, 128)],
        wide.at[:, pl.ds(0, 128)],
    ]
    opposite = [1, 0, 3, 2]
    halos = [
        pltpu.make_async_remote_copy(
            src_ref=halo_from[d],
            dst_ref=halo_to[d],
            send_sem=halo_send.at[d],
            recv_sem=halo_recv.at[d],
            device_id=places[d],
            device_id_type=MESH,
        )
        for d in range(4)
    ]
    for d in range(4):
        pl.when(there[d])(halos[d].start)
    for c in range(MIDDLE, len(chunks)):
        for copy in bulks[c]:
            copy.start()

    full = ifgs * SUB
    rows_of = as_bf16(iota((epochs * SUB, epochs), 0) // SUB == iota((epochs * SUB, epochs), 1))
    tall_inverse = dot(rows_of, inverse[...]).astype(jnp.bfloat16)
    for s in range(n_grp):
        source = lax.rem(grp + n_grp - s, n_grp)
        spot = as_bf16(iota((ifgs, depth), 0) == source * share + iota((ifgs, depth), 1) // SUB)
        same = (iota((epochs * SUB, depth), 0) & (SUB - 1)) == (
            iota((epochs * SUB, depth), 1) & (SUB - 1)
        )
        weights[:, pl.ds(s * depth, depth)] = jnp.where(same, dot(tall_inverse, spot), 0.0).astype(
            jnp.bfloat16
        )

    def series(c):
        y, x = chunks[c]
        for copy in bulks[c]:
            copy.wait_recv()
        data = stack[:, :, pl.ds(y, SUB), pl.ds(x, half)].reshape(full, half)
        out = dot(weights[...], data).reshape(epochs, SUB, half)
        disp[:, pl.ds(y, SUB), pl.ds(x, half)] = out.astype(jnp.bfloat16)
        write(
            disp.at[:, pl.ds(y, SUB), pl.ds(x, half)],
            disp_hbm.at[:, pl.ds(y, SUB), pl.ds(x, half)],
        )

    writes = []

    def write(source, target):
        writes.append(pltpu.make_async_copy(source, target, out_sem.at[len(writes)]))
        writes[-1].start()

    for c in range(EARLY):
        series(c)

    for d in range(4):
        pl.when(there[d])(halos[d].wait_send)
        pl.when(there[opposite[d]])(halos[d].wait_recv)

        @pl.when(jnp.logical_not(there[opposite[d]]))
        def _(d=d):
            halo_to[d][...] = jnp.zeros(halo_to[d].shape, jnp.float32)
    scale = 1.0 / (float(REACH * (REACH + 1) * (2 * REACH + 1) // 3) ** 0.5)
    shape = (tile_rows, tile_rows + 2 * REACH)
    k = iota(shape, 1) - REACH - iota(shape, 0)
    taps = jnp.where(jnp.abs(k) <= REACH, k, 0).astype(jnp.float32).astype(jnp.bfloat16)
    total = None
    for part in parts_of(tall[...]):
        term = dot(taps, part)
        total = term if total is None else total + term
    grad_rows[...] = total * scale
    shape = (tile_cols + 256, tile_cols)
    k = iota(shape, 0) - 128 - iota(shape, 1)
    taps = jnp.where(jnp.abs(k) <= REACH, k, 0).astype(jnp.float32).astype(jnp.bfloat16)
    total = None
    for part in parts_of(wide[...]):
        term = dot(part, taps)
        total = term if total is None else total + term
    grad_cols[...] = total * scale
    write(grad_rows, grad_rows_hbm)
    write(grad_cols, grad_cols_hbm)

    for c in range(EARLY, len(chunks)):
        series(c)
    for c in range(len(chunks)):
        for copy in bulks[c]:
            copy.wait_send()
    for copy in rates:
        copy.wait_send()
    for copy in writes:
        copy.wait()


def write_out(disp, grad_rows, grad_cols, disp_hbm, grad_rows_hbm, grad_cols_hbm, *scratch):
    held, held_rows, held_cols, in_sem, out_sem = scratch
    size = disp.shape[0] // PIECES
    moves = []
    for i in range(PIECES):
        part = pl.ds(i * size, size)
        moves.append((disp.at[part], held.at[part], disp_hbm.at[part]))
    moves.append((grad_rows, held_rows, grad_rows_hbm))
    moves.append((grad_cols, held_cols, grad_cols_hbm))
    reads = [pltpu.make_async_copy(a, b, in_sem.at[i]) for i, (a, b, c) in enumerate(moves)]
    stores = [pltpu.make_async_copy(b, c, out_sem.at[i]) for i, (a, b, c) in enumerate(moves)]
    for read in reads:
        read.start()
    for read, store in zip(reads, stores):
        read.wait()
        store.start()
    for store in stores:
        store.wait()


def on_device(sizes, phase, pseudo_inverse, rotation, plate_id, coherent):
    share, n_grp, tile_rows, tile_cols = phase.shape
    epochs, ifgs = pseudo_inverse.shape
    hbm = pl.BlockSpec(memory_space=pltpu.HBM)
    f32, bf16 = jnp.float32, jnp.bfloat16
    others = n_grp - 1
    chunks = (tile_rows // SUB) * 2
    dma = pltpu.SemaphoreType.DMA
    results = pl.pallas_call(
        functools.partial(kernel, sizes),
        out_shape=(
            jax.ShapeDtypeStruct((epochs, tile_rows, tile_cols), bf16),
            jax.ShapeDtypeStruct((tile_rows, tile_cols), f32),
            jax.ShapeDtypeStruct((tile_rows, tile_cols), f32),
        ),
        in_specs=[
            hbm, hbm, hbm, hbm, hbm,
        ],
        out_specs=(hbm, hbm, hbm),
        scratch_shapes=[
            pltpu.VMEM((epochs, tile_rows, tile_cols), bf16),
            pltpu.VMEM((tile_rows, tile_cols), f32),
            pltpu.VMEM((tile_rows, tile_cols), f32),
            pltpu.VMEM((n_grp, share, tile_rows, tile_cols), bf16),
            pltpu.VMEM((others, share, tile_rows, tile_cols), bf16),
            pltpu.VMEM((epochs, ifgs), bf16),
            pltpu.SMEM(rotation.shape, f32),
            pltpu.VMEM((tile_rows, tile_cols), jnp.int32),
            pltpu.VMEM((tile_rows, tile_cols), jnp.int32),
            pltpu.VMEM((epochs * SUB, ifgs * SUB), bf16),
            pltpu.VMEM((n_grp, tile_rows, tile_cols), f32),
            pltpu.VMEM((others, tile_rows, tile_cols), f32),
            pltpu.VMEM((tile_rows + 2 * REACH, tile_cols), f32),
            pltpu.VMEM((tile_rows, tile_cols + 256), f32),
            dma((4 + n_grp,)),
            dma((others, chunks)),
            dma((others, chunks)),
            dma((others,)),
            dma((others,)),
            dma((4,)),
            dma((4,)),
            dma((chunks + 2,)),
        ],
        compiler_params=pltpu.CompilerParams(
            collective_id=0, has_side_effects=True, vmem_limit_bytes=GRANT
        ),
        cost_estimate=pl.CostEstimate(
            flops=2 * epochs * ifgs * SUB * tile_rows * tile_cols,
            bytes_accessed=8 * 1024 * 1024,
            transcendentals=0,
        ),
    )(phase, pseudo_inverse, rotation, plate_id, coherent)
    return pl.pallas_call(
        write_out,
        out_shape=tuple(jax.ShapeDtypeStruct(r.shape, r.dtype) for r in results),
        in_specs=[hbm] * 3,
        out_specs=(hbm,) * 3,
        scratch_shapes=[pltpu.VMEM(r.shape, r.dtype) for r in results]
        + [dma((PIECES + 2,)), dma((PIECES + 2,))],
        compiler_params=pltpu.CompilerParams(vmem_limit_bytes=GRANT),
    )(*results)


def solution(mesh):
    sizes = (mesh.shape["grp"], mesh.shape["row"], mesh.shape["col"])
    return jax.shard_map(
        functools.partial(on_device, sizes),
        mesh=mesh,
        in_specs=(
            P("grp", None, "row", "col"),
            P(),
            P(),
            P(("grp", "row"), "col"),
            P(("grp", "row"), "col"),
        ),
        out_specs=(
            P(None, ("grp", "row"), "col"),
            P(("grp", "row"), "col"),
            P(("grp", "row"), "col"),
        ),
        check_vma=False,
    )
```

```python
import functools

import jax
import jax.numpy as jnp
from jax import lax
from jax.experimental import pallas as pl
from jax.experimental.pallas import tpu as pltpu
from jax.sharding import PartitionSpec as P

MESH = pl.DeviceIdType.MESH
REACH = 16
SUB = 16
SPLITS = 3
GRANT = 63 * 1024 * 1024
PIECES = 12
EARLY, MIDDLE = 1, 3


def iota(shape, dim):
    return lax.broadcasted_iota(jnp.int32, shape, dim)


def parts_of(value):
    high = value.astype(jnp.bfloat16)
    rest = value - high.astype(jnp.float32)
    middle = rest.astype(jnp.bfloat16)
    low = (rest - middle.astype(jnp.float32)).astype(jnp.bfloat16)
    return high, middle, low


def dot(a, b):
    return jnp.dot(a, b, preferred_element_type=jnp.float32)


def as_bf16(mask):
    return jnp.where(mask, 1.0, 0.0).astype(jnp.bfloat16)


def chunks_of(tile_rows, tile_cols):
    half, quarter = tile_cols // 2, tile_cols // 4
    chunks = [(y, x, half) for y in range(0, tile_rows, SUB) for x in (0, half)]
    y, x, _ = chunks.pop()
    return chunks + [(y, x, quarter), (y, x + quarter, quarter)]


def kernel(
    sizes, phase, inverse_hbm, rotation_hbm, plate_hbm, coherent_hbm,
    disp_hbm, grad_rows_hbm, grad_cols_hbm,
    disp, grad_rows, grad_cols, stack, mine, inverse, rotation, plate, coherent, weights, partial, incoming, tall, wide,
    local_sem, bulk_send, bulk_recv, rate_send, rate_recv, halo_send, halo_recv, out_sem,
):
    n_grp, n_row, n_col = sizes
    _, share, tile_rows, tile_cols = stack.shape
    epochs, ifgs = inverse.shape
    grp, row, col = lax.axis_index("grp"), lax.axis_index("row"), lax.axis_index("col")
    tile = grp * n_row + row
    tiles = n_grp * n_row

    locals_ = [
        pltpu.make_async_copy(inverse_hbm, inverse, local_sem.at[0]),
        pltpu.make_async_copy(plate_hbm, plate, local_sem.at[1]),
        pltpu.make_async_copy(coherent_hbm, coherent, local_sem.at[2]),
        pltpu.make_async_copy(phase.at[:, grp], stack.at[0], local_sem.at[3]),
        pltpu.make_async_copy(rotation_hbm, rotation, local_sem.at[4]),
    ]
    targets = [lax.rem(grp + s, n_grp) for s in range(n_grp)]
    for s in range(1, n_grp):
        locals_.append(
            pltpu.make_async_copy(phase.at[:, targets[s]], mine.at[s - 1], local_sem.at[4 + s])
        )
    for copy in locals_:
        copy.start()

    above, below = tile - 1, tile + 1
    places = [
        {"grp": lax.div(jnp.maximum(above, 0), n_row), "row": lax.rem(jnp.maximum(above, 0), n_row)},
        {"grp": lax.rem(lax.div(below, n_row), n_grp), "row": lax.rem(below, n_row)},
        {"col": jnp.maximum(col - 1, 0)},
        {"col": jnp.minimum(col + 1, n_col - 1)},
    ]
    there = [tile > 0, tile < tiles - 1, col > 0, col < n_col - 1]

    barrier = pltpu.get_barrier_semaphore()
    for s in range(1, n_grp):
        pl.semaphore_signal(barrier, inc=1, device_id={"grp": targets[s]}, device_id_type=MESH)
    for place, exists in zip(places, there):
        @pl.when(exists)
        def _(place=place):
            pl.semaphore_signal(barrier, inc=1, device_id=place, device_id_type=MESH)
    peers = n_grp - 1
    for exists in there:
        peers = peers + jnp.where(exists, 1, 0)
    pl.semaphore_wait(barrier, peers)

    chunks = chunks_of(tile_rows, tile_cols)

    def bulk(s, c):
        y, x, width = chunks[c]
        return pltpu.make_async_remote_copy(
            src_ref=phase.at[:, targets[s], pl.ds(y, SUB), pl.ds(x, width)],
            dst_ref=stack.at[s, :, pl.ds(y, SUB), pl.ds(x, width)],
            send_sem=bulk_send.at[s - 1, c],
            recv_sem=bulk_recv.at[s - 1, c],
            device_id={"grp": targets[s]},
            device_id_type=MESH,
        )

    bulks = [[bulk(s, c) for s in range(1, n_grp)] for c in range(len(chunks))]
    for c in range(EARLY):
        for copy in bulks[c]:
            copy.start()

    locals_[0].wait()
    steps = iota((epochs, 1), 0).astype(jnp.float32) - (epochs - 1) / 2.0
    slope = steps / jnp.sqrt(jnp.sum(steps * steps, axis=0, keepdims=True))
    rate_weight = jnp.sum(inverse[...].astype(jnp.float32) * slope, axis=0, keepdims=True)
    high, middle, low = parts_of(rate_weight)
    pick = iota((SPLITS * SUB, ifgs), 0) // SUB
    spread = jnp.where(
        pick == 0,
        high.astype(jnp.float32),
        jnp.where(pick == 1, middle.astype(jnp.float32), low.astype(jnp.float32)),
    ).astype(jnp.bfloat16)
    depth = share * SUB
    own = as_bf16(iota((ifgs, depth), 0) == grp * share + iota((ifgs, depth), 1) // SUB)
    diagonal = (iota((SPLITS * SUB, depth), 0) & (SUB - 1)) == (
        iota((SPLITS * SUB, depth), 1) & (SUB - 1)
    )
    rate_matrix = jnp.where(diagonal, dot(spread, own), 0.0).astype(jnp.bfloat16)

    def partial_rate(block, slot):
        for y in range(0, tile_rows, SUB):
            data = block[:, pl.ds(y, SUB), :].reshape(depth, tile_cols)
            three = dot(rate_matrix, data)
            partial[slot, pl.ds(y, SUB), :] = (
                three[:SUB] + three[SUB:2 * SUB] + three[2 * SUB:]
            )

    rates = []
    for s in range(1, n_grp):
        locals_[4 + s].wait()
        partial_rate(mine.at[s - 1], s)
        rates.append(
            pltpu.make_async_remote_copy(
                src_ref=partial.at[s],
                dst_ref=incoming.at[s - 1],
                send_sem=rate_send.at[s - 1],
                recv_sem=rate_recv.at[s - 1],
                device_id={"grp": targets[s]},
                device_id_type=MESH,
            )
        )
        rates[-1].start()
    for c in range(EARLY, MIDDLE):
        for copy in bulks[c]:
            copy.start()
    locals_[3].wait()
    partial_rate(stack.at[0], 0)

    locals_[1].wait()
    locals_[2].wait()
    locals_[4].wait()
    ys = (tile * tile_rows + iota((tile_rows, 128), 0)).astype(jnp.float32)
    xs = (col * tile_cols + iota((8, tile_cols), 1)).astype(jnp.float32)
    lat = jnp.deg2rad(36.0 + 6.0 * (ys + 0.5) / (tiles * tile_rows))
    lon = jnp.deg2rad(26.0 + 19.0 * (xs + 0.5) / (n_col * tile_cols))
    cos_lat, sin_lat = jnp.cos(lat)[:, :1], jnp.sin(lat)[:, :1]
    cos_lon, sin_lon = jnp.cos(lon)[:1], jnp.sin(lon)[:1]
    px, py = cos_lat * cos_lon, cos_lat * sin_lon
    pz = sin_lat + jnp.zeros_like(px)
    sx, sy, sz = (0.38, -0.08, 0.92)
    lever = (py * sz - pz * sy, pz * sx - px * sz, px * sy - py * sx)
    plate_rate = jnp.zeros((tile_rows, tile_cols), jnp.float32)
    for p in range(rotation.shape[0]):
        along = rotation[p, 0] * lever[0] + rotation[p, 1] * lever[1] + rotation[p, 2] * lever[2]
        plate_rate = jnp.where(plate[...] == p, along, plate_rate)

    rate = partial[0]
    for s in range(1, n_grp):
        rates[s - 1].wait_recv()
        rate = rate + incoming[s - 1]
    velocity = coherent[...].astype(jnp.float32) * rate - plate_rate
    tall[pl.ds(REACH, tile_rows), :] = velocity
    wide[:, pl.ds(128, tile_cols)] = velocity

    halo_from = [
        tall.at[pl.ds(REACH, REACH), :],
        tall.at[pl.ds(tile_rows, REACH), :],
        wide.at[:, pl.ds(128, 128)],
        wide.at[:, pl.ds(tile_cols, 128)],
    ]
    halo_to = [
        tall.at[pl.ds(REACH + tile_rows, REACH), :],
        tall.at[pl.ds(0, REACH), :],
        wide.at[:, pl.ds(128 + tile_cols, 128)],
        wide.at[:, pl.ds(0, 128)],
    ]
    opposite = [1, 0, 3, 2]
    halos = [
        pltpu.make_async_remote_copy(
            src_ref=halo_from[d],
            dst_ref=halo_to[d],
            send_sem=halo_send.at[d],
            recv_sem=halo_recv.at[d],
            device_id=places[d],
            device_id_type=MESH,
        )
        for d in range(4)
    ]
    for d in range(4):
        pl.when(there[d])(halos[d].start)
    for c in range(MIDDLE, len(chunks)):
        for copy in bulks[c]:
            copy.start()

    full = ifgs * SUB
    rows_of = as_bf16(iota((epochs * SUB, epochs), 0) // SUB == iota((epochs * SUB, epochs), 1))
    tall_inverse = dot(rows_of, inverse[...]).astype(jnp.bfloat16)
    for s in range(n_grp):
        source = lax.rem(grp + n_grp - s, n_grp)
        spot = as_bf16(iota((ifgs, depth), 0) == source * share + iota((ifgs, depth), 1) // SUB)
        same = (iota((epochs * SUB, depth), 0) & (SUB - 1)) == (
            iota((epochs * SUB, depth), 1) & (SUB - 1)
        )
        weights[:, pl.ds(s * depth, depth)] = jnp.where(same, dot(tall_inverse, spot), 0.0).astype(
            jnp.bfloat16
        )

    def series(c):
        y, x, width = chunks[c]
        for copy in bulks[c]:
            copy.wait_recv()
        data = stack[:, :, pl.ds(y, SUB), pl.ds(x, width)].reshape(full, width)
        out = dot(weights[...], data).reshape(epochs, SUB, width)
        disp[:, pl.ds(y, SUB), pl.ds(x, width)] = out.astype(jnp.bfloat16)
        write(
            disp.at[:, pl.ds(y, SUB), pl.ds(x, width)],
            disp_hbm.at[:, pl.ds(y, SUB), pl.ds(x, width)],
        )

    writes = []

    def write(source, target):
        writes.append(pltpu.make_async_copy(source, target, out_sem.at[len(writes)]))
        writes[-1].start()

    for c in range(EARLY):
        series(c)

    for d in range(4):
        pl.when(there[d])(halos[d].wait_send)
        pl.when(there[opposite[d]])(halos[d].wait_recv)

        @pl.when(jnp.logical_not(there[opposite[d]]))
        def _(d=d):
            halo_to[d][...] = jnp.zeros(halo_to[d].shape, jnp.float32)
    scale = 1.0 / (float(REACH * (REACH + 1) * (2 * REACH + 1) // 3) ** 0.5)
    shape = (tile_rows, tile_rows + 2 * REACH)
    k = iota(shape, 1) - REACH - iota(shape, 0)
    taps = jnp.where(jnp.abs(k) <= REACH, k, 0).astype(jnp.float32).astype(jnp.bfloat16)
    total = None
    for part in parts_of(tall[...]):
        term = dot(taps, part)
        total = term if total is None else total + term
    grad_rows[...] = total * scale
    shape = (tile_cols + 256, tile_cols)
    k = iota(shape, 0) - 128 - iota(shape, 1)
    taps = jnp.where(jnp.abs(k) <= REACH, k, 0).astype(jnp.float32).astype(jnp.bfloat16)
    total = None
    for part in parts_of(wide[...]):
        term = dot(part, taps)
        total = term if total is None else total + term
    grad_cols[...] = total * scale
    write(grad_rows, grad_rows_hbm)
    write(grad_cols, grad_cols_hbm)

    for c in range(EARLY, len(chunks)):
        series(c)
    for c in range(len(chunks)):
        for copy in bulks[c]:
            copy.wait_send()
    for copy in rates:
        copy.wait_send()
    for copy in writes:
        copy.wait()


def write_out(disp, grad_rows, grad_cols, disp_hbm, grad_rows_hbm, grad_cols_hbm, *scratch):
    held, held_rows, held_cols, in_sem, out_sem = scratch
    size = disp.shape[0] // PIECES
    moves = []
    for i in range(PIECES):
        part = pl.ds(i * size, size)
        moves.append((disp.at[part], held.at[part], disp_hbm.at[part]))
    moves.append((grad_rows, held_rows, grad_rows_hbm))
    moves.append((grad_cols, held_cols, grad_cols_hbm))
    reads = [pltpu.make_async_copy(a, b, in_sem.at[i]) for i, (a, b, c) in enumerate(moves)]
    stores = [pltpu.make_async_copy(b, c, out_sem.at[i]) for i, (a, b, c) in enumerate(moves)]
    for read in reads:
        read.start()
    for read, store in zip(reads, stores):
        read.wait()
        store.start()
    for store in stores:
        store.wait()


def on_device(sizes, phase, pseudo_inverse, rotation, plate_id, coherent):
    share, n_grp, tile_rows, tile_cols = phase.shape
    epochs, ifgs = pseudo_inverse.shape
    hbm = pl.BlockSpec(memory_space=pltpu.HBM)
    f32, bf16 = jnp.float32, jnp.bfloat16
    others = n_grp - 1
    chunks = len(chunks_of(tile_rows, tile_cols))
    dma = pltpu.SemaphoreType.DMA
    results = pl.pallas_call(
        functools.partial(kernel, sizes),
        out_shape=(
            jax.ShapeDtypeStruct((epochs, tile_rows, tile_cols), bf16),
            jax.ShapeDtypeStruct((tile_rows, tile_cols), f32),
            jax.ShapeDtypeStruct((tile_rows, tile_cols), f32),
        ),
        in_specs=[
            hbm, hbm, hbm, hbm, hbm,
        ],
        out_specs=(hbm, hbm, hbm),
        scratch_shapes=[
            pltpu.VMEM((epochs, tile_rows, tile_cols), bf16),
            pltpu.VMEM((tile_rows, tile_cols), f32),
            pltpu.VMEM((tile_rows, tile_cols), f32),
            pltpu.VMEM((n_grp, share, tile_rows, tile_cols), bf16),
            pltpu.VMEM((others, share, tile_rows, tile_cols), bf16),
            pltpu.VMEM((epochs, ifgs), bf16),
            pltpu.SMEM(rotation.shape, f32),
            pltpu.VMEM((tile_rows, tile_cols), jnp.int32),
            pltpu.VMEM((tile_rows, tile_cols), jnp.int32),
            pltpu.VMEM((epochs * SUB, ifgs * SUB), bf16),
            pltpu.VMEM((n_grp, tile_rows, tile_cols), f32),
            pltpu.VMEM((others, tile_rows, tile_cols), f32),
            pltpu.VMEM((tile_rows + 2 * REACH, tile_cols), f32),
            pltpu.VMEM((tile_rows, tile_cols + 256), f32),
            dma((4 + n_grp,)),
            dma((others, chunks)),
            dma((others, chunks)),
            dma((others,)),
            dma((others,)),
            dma((4,)),
            dma((4,)),
            dma((chunks + 2,)),
        ],
        compiler_params=pltpu.CompilerParams(
            collective_id=0, has_side_effects=True, vmem_limit_bytes=GRANT
        ),
        cost_estimate=pl.CostEstimate(
            flops=2 * epochs * ifgs * SUB * tile_rows * tile_cols,
            bytes_accessed=8 * 1024 * 1024,
            transcendentals=0,
        ),
    )(phase, pseudo_inverse, rotation, plate_id, coherent)
    return pl.pallas_call(
        write_out,
        out_shape=tuple(jax.ShapeDtypeStruct(r.shape, r.dtype) for r in results),
        in_specs=[hbm] * 3,
        out_specs=(hbm,) * 3,
        scratch_shapes=[pltpu.VMEM(r.shape, r.dtype) for r in results]
        + [dma((PIECES + 2,)), dma((PIECES + 2,))],
        compiler_params=pltpu.CompilerParams(vmem_limit_bytes=GRANT),
    )(*results)


def solution(mesh):
    sizes = (mesh.shape["grp"], mesh.shape["row"], mesh.shape["col"])
    return jax.shard_map(
        functools.partial(on_device, sizes),
        mesh=mesh,
        in_specs=(
            P("grp", None, "row", "col"),
            P(),
            P(),
            P(("grp", "row"), "col"),
            P(("grp", "row"), "col"),
        ),
        out_specs=(
            P(None, ("grp", "row"), "col"),
            P(("grp", "row"), "col"),
            P(("grp", "row"), "col"),
        ),
        check_vma=False,
    )
```

```python
import functools

import jax
import jax.numpy as jnp
from jax import lax
from jax.experimental import pallas as pl
from jax.experimental.pallas import tpu as pltpu
from jax.sharding import PartitionSpec as P

MESH = pl.DeviceIdType.MESH
REACH = 16
SUB = 16
SPLITS = 3
GRANT = 63 * 1024 * 1024
PIECES = 12
PARTS = 4
EARLY, MIDDLE = 2, 6


def iota(shape, dim):
    return lax.broadcasted_iota(jnp.int32, shape, dim)


def parts_of(value):
    high = value.astype(jnp.bfloat16)
    rest = value - high.astype(jnp.float32)
    middle = rest.astype(jnp.bfloat16)
    low = (rest - middle.astype(jnp.float32)).astype(jnp.bfloat16)
    return high, middle, low


def dot(a, b):
    return jnp.dot(a, b, preferred_element_type=jnp.float32)


def as_bf16(mask):
    return jnp.where(mask, 1.0, 0.0).astype(jnp.bfloat16)


def chunks_of(share, tile_rows):
    size = share // PARTS
    return [(y, i * size, size) for y in range(0, tile_rows, SUB) for i in range(PARTS)]


def kernel(
    sizes, phase, inverse_hbm, rotation_hbm, plate_hbm, coherent_hbm,
    disp_hbm, grad_rows_hbm, grad_cols_hbm,
    disp, grad_rows, grad_cols, stack, mine, inverse, rotation, plate, coherent, weights, partial, incoming, tall, wide,
    local_sem, bulk_send, bulk_recv, rate_send, rate_recv, halo_send, halo_recv, out_sem,
):
    n_grp, n_row, n_col = sizes
    _, share, tile_rows, tile_cols = stack.shape
    epochs, ifgs = inverse.shape
    grp, row, col = lax.axis_index("grp"), lax.axis_index("row"), lax.axis_index("col")
    tile = grp * n_row + row
    tiles = n_grp * n_row

    locals_ = [
        pltpu.make_async_copy(inverse_hbm, inverse, local_sem.at[0]),
        pltpu.make_async_copy(plate_hbm, plate, local_sem.at[1]),
        pltpu.make_async_copy(coherent_hbm, coherent, local_sem.at[2]),
        pltpu.make_async_copy(phase.at[:, grp], stack.at[0], local_sem.at[3]),
        pltpu.make_async_copy(rotation_hbm, rotation, local_sem.at[4]),
    ]
    targets = [lax.rem(grp + s, n_grp) for s in range(n_grp)]
    for s in range(1, n_grp):
        locals_.append(
            pltpu.make_async_copy(phase.at[:, targets[s]], mine.at[s - 1], local_sem.at[4 + s])
        )
    for copy in locals_:
        copy.start()

    above, below = tile - 1, tile + 1
    places = [
        {"grp": lax.div(jnp.maximum(above, 0), n_row), "row": lax.rem(jnp.maximum(above, 0), n_row)},
        {"grp": lax.rem(lax.div(below, n_row), n_grp), "row": lax.rem(below, n_row)},
        {"col": jnp.maximum(col - 1, 0)},
        {"col": jnp.minimum(col + 1, n_col - 1)},
    ]
    there = [tile > 0, tile < tiles - 1, col > 0, col < n_col - 1]

    barrier = pltpu.get_barrier_semaphore()
    for s in range(1, n_grp):
        pl.semaphore_signal(barrier, inc=1, device_id={"grp": targets[s]}, device_id_type=MESH)
    for place, exists in zip(places, there):
        @pl.when(exists)
        def _(place=place):
            pl.semaphore_signal(barrier, inc=1, device_id=place, device_id_type=MESH)
    peers = n_grp - 1
    for exists in there:
        peers = peers + jnp.where(exists, 1, 0)
    pl.semaphore_wait(barrier, peers)

    chunks = chunks_of(share, tile_rows)

    def bulk(s, c):
        y, first, size = chunks[c]
        part = pl.ds(first, size)
        return pltpu.make_async_remote_copy(
            src_ref=phase.at[part, targets[s], pl.ds(y, SUB), :],
            dst_ref=stack.at[s, part, pl.ds(y, SUB), :],
            send_sem=bulk_send.at[s - 1, c],
            recv_sem=bulk_recv.at[s - 1, c],
            device_id={"grp": targets[s]},
            device_id_type=MESH,
        )

    bulks = [[bulk(s, c) for s in range(1, n_grp)] for c in range(len(chunks))]
    for c in range(EARLY):
        for copy in bulks[c]:
            copy.start()

    locals_[0].wait()
    steps = iota((epochs, 1), 0).astype(jnp.float32) - (epochs - 1) / 2.0
    slope = steps / jnp.sqrt(jnp.sum(steps * steps, axis=0, keepdims=True))
    rate_weight = jnp.sum(inverse[...].astype(jnp.float32) * slope, axis=0, keepdims=True)
    high, middle, low = parts_of(rate_weight)
    pick = iota((SPLITS * SUB, ifgs), 0) // SUB
    spread = jnp.where(
        pick == 0,
        high.astype(jnp.float32),
        jnp.where(pick == 1, middle.astype(jnp.float32), low.astype(jnp.float32)),
    ).astype(jnp.bfloat16)
    depth = share * SUB
    own = as_bf16(iota((ifgs, depth), 0) == grp * share + iota((ifgs, depth), 1) // SUB)
    diagonal = (iota((SPLITS * SUB, depth), 0) & (SUB - 1)) == (
        iota((SPLITS * SUB, depth), 1) & (SUB - 1)
    )
    rate_matrix = jnp.where(diagonal, dot(spread, own), 0.0).astype(jnp.bfloat16)

    def partial_rate(block, slot):
        for y in range(0, tile_rows, SUB):
            data = block[:, pl.ds(y, SUB), :].reshape(depth, tile_cols)
            three = dot(rate_matrix, data)
            partial[slot, pl.ds(y, SUB), :] = (
                three[:SUB] + three[SUB:2 * SUB] + three[2 * SUB:]
            )

    rates = []
    for s in range(1, n_grp):
        locals_[4 + s].wait()
        partial_rate(mine.at[s - 1], s)
        rates.append(
            pltpu.make_async_remote_copy(
                src_ref=partial.at[s],
                dst_ref=incoming.at[s - 1],
                send_sem=rate_send.at[s - 1],
                recv_sem=rate_recv.at[s - 1],
                device_id={"grp": targets[s]},
                device_id_type=MESH,
            )
        )
        rates[-1].start()
    for c in range(EARLY, MIDDLE):
        for copy in bulks[c]:
            copy.start()
    locals_[3].wait()
    partial_rate(stack.at[0], 0)

    locals_[1].wait()
    locals_[2].wait()
    locals_[4].wait()
    ys = (tile * tile_rows + iota((tile_rows, 128), 0)).astype(jnp.float32)
    xs = (col * tile_cols + iota((8, tile_cols), 1)).astype(jnp.float32)
    lat = jnp.deg2rad(36.0 + 6.0 * (ys + 0.5) / (tiles * tile_rows))
    lon = jnp.deg2rad(26.0 + 19.0 * (xs + 0.5) / (n_col * tile_cols))
    cos_lat, sin_lat = jnp.cos(lat)[:, :1], jnp.sin(lat)[:, :1]
    cos_lon, sin_lon = jnp.cos(lon)[:1], jnp.sin(lon)[:1]
    px, py = cos_lat * cos_lon, cos_lat * sin_lon
    pz = sin_lat + jnp.zeros_like(px)
    sx, sy, sz = (0.38, -0.08, 0.92)
    lever = (py * sz - pz * sy, pz * sx - px * sz, px * sy - py * sx)
    plate_rate = jnp.zeros((tile_rows, tile_cols), jnp.float32)
    for p in range(rotation.shape[0]):
        along = rotation[p, 0] * lever[0] + rotation[p, 1] * lever[1] + rotation[p, 2] * lever[2]
        plate_rate = jnp.where(plate[...] == p, along, plate_rate)

    rate = partial[0]
    for s in range(1, n_grp):
        rates[s - 1].wait_recv()
        rate = rate + incoming[s - 1]
    velocity = coherent[...].astype(jnp.float32) * rate - plate_rate
    tall[pl.ds(REACH, tile_rows), :] = velocity
    wide[:, pl.ds(128, tile_cols)] = velocity

    halo_from = [
        tall.at[pl.ds(REACH, REACH), :],
        tall.at[pl.ds(tile_rows, REACH), :],
        wide.at[:, pl.ds(128, 128)],
        wide.at[:, pl.ds(tile_cols, 128)],
    ]
    halo_to = [
        tall.at[pl.ds(REACH + tile_rows, REACH), :],
        tall.at[pl.ds(0, REACH), :],
        wide.at[:, pl.ds(128 + tile_cols, 128)],
        wide.at[:, pl.ds(0, 128)],
    ]
    opposite = [1, 0, 3, 2]
    halos = [
        pltpu.make_async_remote_copy(
            src_ref=halo_from[d],
            dst_ref=halo_to[d],
            send_sem=halo_send.at[d],
            recv_sem=halo_recv.at[d],
            device_id=places[d],
            device_id_type=MESH,
        )
        for d in range(4)
    ]
    for d in range(4):
        pl.when(there[d])(halos[d].start)
    for c in range(MIDDLE, len(chunks)):
        for copy in bulks[c]:
            copy.start()

    full = ifgs * SUB
    rows_of = as_bf16(iota((epochs * SUB, epochs), 0) // SUB == iota((epochs * SUB, epochs), 1))
    tall_inverse = dot(rows_of, inverse[...]).astype(jnp.bfloat16)
    for s in range(n_grp):
        source = lax.rem(grp + n_grp - s, n_grp)
        spot = as_bf16(iota((ifgs, depth), 0) == source * share + iota((ifgs, depth), 1) // SUB)
        same = (iota((epochs * SUB, depth), 0) & (SUB - 1)) == (
            iota((epochs * SUB, depth), 1) & (SUB - 1)
        )
        weights[:, pl.ds(s * depth, depth)] = jnp.where(same, dot(tall_inverse, spot), 0.0).astype(
            jnp.bfloat16
        )

    def series(group):
        for c in range(group * PARTS, (group + 1) * PARTS):
            for copy in bulks[c]:
                copy.wait_recv()
        rows = pl.ds(group * SUB, SUB)
        width = tile_cols // 2
        for x in range(0, tile_cols, width):
            cols = pl.ds(x, width)
            data = stack[:, :, rows, cols].reshape(full, width)
            out = dot(weights[...], data).reshape(epochs, SUB, width)
            disp[:, rows, cols] = out.astype(jnp.bfloat16)
            write(disp.at[:, rows, cols], disp_hbm.at[:, rows, cols])

    writes = []

    def write(source, target):
        writes.append(pltpu.make_async_copy(source, target, out_sem.at[len(writes)]))
        writes[-1].start()

    groups = tile_rows // SUB
    for group in range(groups - 1):
        series(group)

    for d in range(4):
        pl.when(there[d])(halos[d].wait_send)
        pl.when(there[opposite[d]])(halos[d].wait_recv)

        @pl.when(jnp.logical_not(there[opposite[d]]))
        def _(d=d):
            halo_to[d][...] = jnp.zeros(halo_to[d].shape, jnp.float32)
    scale = 1.0 / (float(REACH * (REACH + 1) * (2 * REACH + 1) // 3) ** 0.5)
    shape = (tile_rows, tile_rows + 2 * REACH)
    k = iota(shape, 1) - REACH - iota(shape, 0)
    taps = jnp.where(jnp.abs(k) <= REACH, k, 0).astype(jnp.float32).astype(jnp.bfloat16)
    total = None
    for part in parts_of(tall[...]):
        term = dot(taps, part)
        total = term if total is None else total + term
    grad_rows[...] = total * scale
    shape = (tile_cols + 256, tile_cols)
    k = iota(shape, 0) - 128 - iota(shape, 1)
    taps = jnp.where(jnp.abs(k) <= REACH, k, 0).astype(jnp.float32).astype(jnp.bfloat16)
    total = None
    for part in parts_of(wide[...]):
        term = dot(part, taps)
        total = term if total is None else total + term
    grad_cols[...] = total * scale
    write(grad_rows, grad_rows_hbm)
    write(grad_cols, grad_cols_hbm)

    series(groups - 1)
    for c in range(len(chunks)):
        for copy in bulks[c]:
            copy.wait_send()
    for copy in rates:
        copy.wait_send()
    for copy in writes:
        copy.wait()


def write_out(disp, grad_rows, grad_cols, disp_hbm, grad_rows_hbm, grad_cols_hbm, *scratch):
    held, held_rows, held_cols, in_sem, out_sem = scratch
    size = disp.shape[0] // PIECES
    moves = []
    for i in range(PIECES):
        part = pl.ds(i * size, size)
        moves.append((disp.at[part], held.at[part], disp_hbm.at[part]))
    moves.append((grad_rows, held_rows, grad_rows_hbm))
    moves.append((grad_cols, held_cols, grad_cols_hbm))
    reads = [pltpu.make_async_copy(a, b, in_sem.at[i]) for i, (a, b, c) in enumerate(moves)]
    stores = [pltpu.make_async_copy(b, c, out_sem.at[i]) for i, (a, b, c) in enumerate(moves)]
    for read in reads:
        read.start()
    for read, store in zip(reads, stores):
        read.wait()
        store.start()
    for store in stores:
        store.wait()


def on_device(sizes, phase, pseudo_inverse, rotation, plate_id, coherent):
    share, n_grp, tile_rows, tile_cols = phase.shape
    epochs, ifgs = pseudo_inverse.shape
    hbm = pl.BlockSpec(memory_space=pltpu.HBM)
    f32, bf16 = jnp.float32, jnp.bfloat16
    others = n_grp - 1
    chunks = len(chunks_of(share, tile_rows))
    dma = pltpu.SemaphoreType.DMA
    results = pl.pallas_call(
        functools.partial(kernel, sizes),
        out_shape=(
            jax.ShapeDtypeStruct((epochs, tile_rows, tile_cols), bf16),
            jax.ShapeDtypeStruct((tile_rows, tile_cols), f32),
            jax.ShapeDtypeStruct((tile_rows, tile_cols), f32),
        ),
        in_specs=[
            hbm, hbm, hbm, hbm, hbm,
        ],
        out_specs=(hbm, hbm, hbm),
        scratch_shapes=[
            pltpu.VMEM((epochs, tile_rows, tile_cols), bf16),
            pltpu.VMEM((tile_rows, tile_cols), f32),
            pltpu.VMEM((tile_rows, tile_cols), f32),
            pltpu.VMEM((n_grp, share, tile_rows, tile_cols), bf16),
            pltpu.VMEM((others, share, tile_rows, tile_cols), bf16),
            pltpu.VMEM((epochs, ifgs), bf16),
            pltpu.SMEM(rotation.shape, f32),
            pltpu.VMEM((tile_rows, tile_cols), jnp.int32),
            pltpu.VMEM((tile_rows, tile_cols), jnp.int32),
            pltpu.VMEM((epochs * SUB, ifgs * SUB), bf16),
            pltpu.VMEM((n_grp, tile_rows, tile_cols), f32),
            pltpu.VMEM((others, tile_rows, tile_cols), f32),
            pltpu.VMEM((tile_rows + 2 * REACH, tile_cols), f32),
            pltpu.VMEM((tile_rows, tile_cols + 256), f32),
            dma((4 + n_grp,)),
            dma((others, chunks)),
            dma((others, chunks)),
            dma((others,)),
            dma((others,)),
            dma((4,)),
            dma((4,)),
            dma((2 * (tile_rows // SUB) + 2,)),
        ],
        compiler_params=pltpu.CompilerParams(
            collective_id=0, has_side_effects=True, vmem_limit_bytes=GRANT
        ),
        cost_estimate=pl.CostEstimate(
            flops=2 * epochs * ifgs * SUB * tile_rows * tile_cols,
            bytes_accessed=8 * 1024 * 1024,
            transcendentals=0,
        ),
    )(phase, pseudo_inverse, rotation, plate_id, coherent)
    return pl.pallas_call(
        write_out,
        out_shape=tuple(jax.ShapeDtypeStruct(r.shape, r.dtype) for r in results),
        in_specs=[hbm] * 3,
        out_specs=(hbm,) * 3,
        scratch_shapes=[pltpu.VMEM(r.shape, r.dtype) for r in results]
        + [dma((PIECES + 2,)), dma((PIECES + 2,))],
        compiler_params=pltpu.CompilerParams(vmem_limit_bytes=GRANT),
    )(*results)


def solution(mesh):
    sizes = (mesh.shape["grp"], mesh.shape["row"], mesh.shape["col"])
    return jax.shard_map(
        functools.partial(on_device, sizes),
        mesh=mesh,
        in_specs=(
            P("grp", None, "row", "col"),
            P(),
            P(),
            P(("grp", "row"), "col"),
            P(("grp", "row"), "col"),
        ),
        out_specs=(
            P(None, ("grp", "row"), "col"),
            P(("grp", "row"), "col"),
            P(("grp", "row"), "col"),
        ),
        check_vma=False,
    )
```

```python
import functools

import jax
import jax.numpy as jnp
from jax import lax
from jax.experimental import pallas as pl
from jax.experimental.pallas import tpu as pltpu
from jax.sharding import PartitionSpec as P

MESH = pl.DeviceIdType.MESH
REACH = 16
SUB = 16
SPLITS = 3
GRANT = 63 * 1024 * 1024
PIECES = 12
EARLY, MIDDLE = 1, 3


def iota(shape, dim):
    return lax.broadcasted_iota(jnp.int32, shape, dim)


def parts_of(value):
    high = value.astype(jnp.bfloat16)
    rest = value - high.astype(jnp.float32)
    middle = rest.astype(jnp.bfloat16)
    low = (rest - middle.astype(jnp.float32)).astype(jnp.bfloat16)
    return high, middle, low


def dot(a, b):
    return jnp.dot(a, b, preferred_element_type=jnp.float32)


def as_bf16(mask):
    return jnp.where(mask, 1.0, 0.0).astype(jnp.bfloat16)


def chunks_of(tile_rows, tile_cols):
    half, quarter = tile_cols // 2, tile_cols // 4
    chunks = [(y, x, half) for y in range(0, tile_rows, SUB) for x in (0, half)]
    y, x, _ = chunks.pop()
    return chunks + [(y, x, quarter), (y, x + quarter, quarter)]


def kernel(
    sizes, phase, inverse_hbm, rotation_hbm, plate_hbm, coherent_hbm,
    disp_hbm, grad_rows_hbm, grad_cols_hbm,
    disp, grad_rows, grad_cols, stack, mine, inverse, rotation, plate, coherent, weights, partial, incoming, tall, wide,
    local_sem, bulk_send, bulk_recv, rate_send, rate_recv, halo_send, halo_recv, out_sem, base,
):
    n_grp, n_row, n_col = sizes
    _, share, tile_rows, tile_cols = stack.shape
    epochs, ifgs = inverse.shape
    grp, row, col = lax.axis_index("grp"), lax.axis_index("row"), lax.axis_index("col")
    tile = grp * n_row + row
    tiles = n_grp * n_row

    locals_ = [
        pltpu.make_async_copy(inverse_hbm, inverse, local_sem.at[0]),
        pltpu.make_async_copy(plate_hbm, plate, local_sem.at[1]),
        pltpu.make_async_copy(coherent_hbm, coherent, local_sem.at[2]),
        pltpu.make_async_copy(phase.at[:, grp], stack.at[0], local_sem.at[3]),
        pltpu.make_async_copy(rotation_hbm, rotation, local_sem.at[4]),
    ]
    targets = [lax.rem(grp + s, n_grp) for s in range(n_grp)]
    for s in range(1, n_grp):
        locals_.append(
            pltpu.make_async_copy(phase.at[:, targets[s]], mine.at[s - 1], local_sem.at[4 + s])
        )
    for copy in locals_:
        copy.start()

    above, below = tile - 1, tile + 1
    places = [
        {"grp": lax.div(jnp.maximum(above, 0), n_row), "row": lax.rem(jnp.maximum(above, 0), n_row)},
        {"grp": lax.rem(lax.div(below, n_row), n_grp), "row": lax.rem(below, n_row)},
        {"col": jnp.maximum(col - 1, 0)},
        {"col": jnp.minimum(col + 1, n_col - 1)},
    ]
    there = [tile > 0, tile < tiles - 1, col > 0, col < n_col - 1]

    barrier = pltpu.get_barrier_semaphore()
    for s in range(1, n_grp):
        pl.semaphore_signal(barrier, inc=1, device_id={"grp": targets[s]}, device_id_type=MESH)
    for place, exists in zip(places, there):
        @pl.when(exists)
        def _(place=place):
            pl.semaphore_signal(barrier, inc=1, device_id=place, device_id_type=MESH)
    peers = n_grp - 1
    for exists in there:
        peers = peers + jnp.where(exists, 1, 0)
    pl.semaphore_wait(barrier, peers)

    chunks = chunks_of(tile_rows, tile_cols)

    def bulk(s, c):
        y, x, width = chunks[c]
        return pltpu.make_async_remote_copy(
            src_ref=phase.at[:, targets[s], pl.ds(y, SUB), pl.ds(x, width)],
            dst_ref=stack.at[s, :, pl.ds(y, SUB), pl.ds(x, width)],
            send_sem=bulk_send.at[s - 1, c],
            recv_sem=bulk_recv.at[s - 1, c],
            device_id={"grp": targets[s]},
            device_id_type=MESH,
        )

    bulks = [[bulk(s, c) for s in range(1, n_grp)] for c in range(len(chunks))]
    for c in range(EARLY):
        for copy in bulks[c]:
            copy.start()

    locals_[0].wait()
    steps = iota((epochs, 1), 0).astype(jnp.float32) - (epochs - 1) / 2.0
    slope = steps / jnp.sqrt(jnp.sum(steps * steps, axis=0, keepdims=True))
    rate_weight = jnp.sum(inverse[...].astype(jnp.float32) * slope, axis=0, keepdims=True)
    high, middle, low = parts_of(rate_weight)
    pick = iota((SPLITS * SUB, ifgs), 0) // SUB
    spread = jnp.where(
        pick == 0,
        high.astype(jnp.float32),
        jnp.where(pick == 1, middle.astype(jnp.float32), low.astype(jnp.float32)),
    ).astype(jnp.bfloat16)
    depth = share * SUB
    own = as_bf16(iota((ifgs, depth), 0) == grp * share + iota((ifgs, depth), 1) // SUB)
    diagonal = (iota((SPLITS * SUB, depth), 0) & (SUB - 1)) == (
        iota((SPLITS * SUB, depth), 1) & (SUB - 1)
    )
    rate_matrix = jnp.where(diagonal, dot(spread, own), 0.0).astype(jnp.bfloat16)

    def partial_rate(block, slot):
        for y in range(0, tile_rows, SUB):
            data = block[:, pl.ds(y, SUB), :].reshape(depth, tile_cols)
            three = dot(rate_matrix, data)
            partial[slot, pl.ds(y, SUB), :] = (
                three[:SUB] + three[SUB:2 * SUB] + three[2 * SUB:]
            )

    rates = []
    for s in range(1, n_grp):
        locals_[4 + s].wait()
        partial_rate(mine.at[s - 1], s)
        rates.append(
            pltpu.make_async_remote_copy(
                src_ref=partial.at[s],
                dst_ref=incoming.at[s - 1],
                send_sem=rate_send.at[s - 1],
                recv_sem=rate_recv.at[s - 1],
                device_id={"grp": targets[s]},
                device_id_type=MESH,
            )
        )
        rates[-1].start()
    for c in range(EARLY, MIDDLE):
        for copy in bulks[c]:
            copy.start()
    locals_[3].wait()
    partial_rate(stack.at[0], 0)

    locals_[1].wait()
    locals_[2].wait()
    locals_[4].wait()
    ys = (tile * tile_rows + iota((tile_rows, 128), 0)).astype(jnp.float32)
    xs = (col * tile_cols + iota((8, tile_cols), 1)).astype(jnp.float32)
    lat = jnp.deg2rad(36.0 + 6.0 * (ys + 0.5) / (tiles * tile_rows))
    lon = jnp.deg2rad(26.0 + 19.0 * (xs + 0.5) / (n_col * tile_cols))
    cos_lat, sin_lat = jnp.cos(lat)[:, :1], jnp.sin(lat)[:, :1]
    cos_lon, sin_lon = jnp.cos(lon)[:1], jnp.sin(lon)[:1]
    px, py = cos_lat * cos_lon, cos_lat * sin_lon
    pz = sin_lat + jnp.zeros_like(px)
    sx, sy, sz = (0.38, -0.08, 0.92)
    lever = (py * sz - pz * sy, pz * sx - px * sz, px * sy - py * sx)
    plate_rate = jnp.zeros((tile_rows, tile_cols), jnp.float32)
    for p in range(rotation.shape[0]):
        along = rotation[p, 0] * lever[0] + rotation[p, 1] * lever[1] + rotation[p, 2] * lever[2]
        plate_rate = jnp.where(plate[...] == p, along, plate_rate)

    rate = partial[0]
    for s in range(1, n_grp):
        rates[s - 1].wait_recv()
        rate = rate + incoming[s - 1]
    velocity = coherent[...].astype(jnp.float32) * rate - plate_rate
    tall[pl.ds(REACH, tile_rows), :] = velocity
    wide[:, pl.ds(128, tile_cols)] = velocity

    halo_from = [
        tall.at[pl.ds(REACH, REACH), :],
        tall.at[pl.ds(tile_rows, REACH), :],
        wide.at[:, pl.ds(128, 128)],
        wide.at[:, pl.ds(tile_cols, 128)],
    ]
    halo_to = [
        tall.at[pl.ds(REACH + tile_rows, REACH), :],
        tall.at[pl.ds(0, REACH), :],
        wide.at[:, pl.ds(128 + tile_cols, 128)],
        wide.at[:, pl.ds(0, 128)],
    ]
    opposite = [1, 0, 3, 2]
    halos = [
        pltpu.make_async_remote_copy(
            src_ref=halo_from[d],
            dst_ref=halo_to[d],
            send_sem=halo_send.at[d],
            recv_sem=halo_recv.at[d],
            device_id=places[d],
            device_id_type=MESH,
        )
        for d in range(4)
    ]
    for d in range(4):
        pl.when(there[d])(halos[d].start)
    for c in range(MIDDLE, len(chunks)):
        for copy in bulks[c]:
            copy.start()

    full = ifgs * SUB
    rows_of = as_bf16(iota((epochs * SUB, epochs), 0) // SUB == iota((epochs * SUB, epochs), 1))
    tall_inverse = dot(rows_of, inverse[...]).astype(jnp.bfloat16)
    for s in range(n_grp):
        source = lax.rem(grp + n_grp - s, n_grp)
        spot = as_bf16(iota((ifgs, depth), 0) == source * share + iota((ifgs, depth), 1) // SUB)
        same = (iota((epochs * SUB, depth), 0) & (SUB - 1)) == (
            iota((epochs * SUB, depth), 1) & (SUB - 1)
        )
        weights[:, pl.ds(s * depth, depth)] = jnp.where(same, dot(tall_inverse, spot), 0.0).astype(
            jnp.bfloat16
        )

    for y, x, width in chunks:
        data = stack[0, :, pl.ds(y, SUB), pl.ds(x, width)].reshape(depth, width)
        base[:, pl.ds(y // SUB * tile_cols + x, width)] = dot(weights[:, :depth], data)

    def series(c):
        y, x, width = chunks[c]
        for copy in bulks[c]:
            copy.wait_recv()
        data = stack[1:, :, pl.ds(y, SUB), pl.ds(x, width)].reshape(full - depth, width)
        out = base[:, pl.ds(y // SUB * tile_cols + x, width)] + dot(weights[:, depth:], data)
        out = out.reshape(epochs, SUB, width)
        disp[:, pl.ds(y, SUB), pl.ds(x, width)] = out.astype(jnp.bfloat16)
        write(
            disp.at[:, pl.ds(y, SUB), pl.ds(x, width)],
            disp_hbm.at[:, pl.ds(y, SUB), pl.ds(x, width)],
        )

    writes = []

    def write(source, target):
        writes.append(pltpu.make_async_copy(source, target, out_sem.at[len(writes)]))
        writes[-1].start()

    for c in range(EARLY):
        series(c)

    for d in range(4):
        pl.when(there[d])(halos[d].wait_send)
        pl.when(there[opposite[d]])(halos[d].wait_recv)

        @pl.when(jnp.logical_not(there[opposite[d]]))
        def _(d=d):
            halo_to[d][...] = jnp.zeros(halo_to[d].shape, jnp.float32)
    scale = 1.0 / (float(REACH * (REACH + 1) * (2 * REACH + 1) // 3) ** 0.5)
    shape = (tile_rows, tile_rows + 2 * REACH)
    k = iota(shape, 1) - REACH - iota(shape, 0)
    taps = jnp.where(jnp.abs(k) <= REACH, k, 0).astype(jnp.float32).astype(jnp.bfloat16)
    total = None
    for part in parts_of(tall[...]):
        term = dot(taps, part)
        total = term if total is None else total + term
    grad_rows[...] = total * scale
    shape = (tile_cols + 256, tile_cols)
    k = iota(shape, 0) - 128 - iota(shape, 1)
    taps = jnp.where(jnp.abs(k) <= REACH, k, 0).astype(jnp.float32).astype(jnp.bfloat16)
    total = None
    for part in parts_of(wide[...]):
        term = dot(part, taps)
        total = term if total is None else total + term
    grad_cols[...] = total * scale
    write(grad_rows, grad_rows_hbm)
    write(grad_cols, grad_cols_hbm)

    for c in range(EARLY, len(chunks)):
        series(c)
    for c in range(len(chunks)):
        for copy in bulks[c]:
            copy.wait_send()
    for copy in rates:
        copy.wait_send()
    for copy in writes:
        copy.wait()


def write_out(disp, grad_rows, grad_cols, disp_hbm, grad_rows_hbm, grad_cols_hbm, *scratch):
    held, held_rows, held_cols, in_sem, out_sem = scratch
    size = disp.shape[0] // PIECES
    moves = []
    for i in range(PIECES):
        part = pl.ds(i * size, size)
        moves.append((disp.at[part], held.at[part], disp_hbm.at[part]))
    moves.append((grad_rows, held_rows, grad_rows_hbm))
    moves.append((grad_cols, held_cols, grad_cols_hbm))
    reads = [pltpu.make_async_copy(a, b, in_sem.at[i]) for i, (a, b, c) in enumerate(moves)]
    stores = [pltpu.make_async_copy(b, c, out_sem.at[i]) for i, (a, b, c) in enumerate(moves)]
    for read in reads:
        read.start()
    for read, store in zip(reads, stores):
        read.wait()
        store.start()
    for store in stores:
        store.wait()


def on_device(sizes, phase, pseudo_inverse, rotation, plate_id, coherent):
    share, n_grp, tile_rows, tile_cols = phase.shape
    epochs, ifgs = pseudo_inverse.shape
    hbm = pl.BlockSpec(memory_space=pltpu.HBM)
    f32, bf16 = jnp.float32, jnp.bfloat16
    others = n_grp - 1
    chunks = len(chunks_of(tile_rows, tile_cols))
    dma = pltpu.SemaphoreType.DMA
    results = pl.pallas_call(
        functools.partial(kernel, sizes),
        out_shape=(
            jax.ShapeDtypeStruct((epochs, tile_rows, tile_cols), bf16),
            jax.ShapeDtypeStruct((tile_rows, tile_cols), f32),
            jax.ShapeDtypeStruct((tile_rows, tile_cols), f32),
        ),
        in_specs=[
            hbm, hbm, hbm, hbm, hbm,
        ],
        out_specs=(hbm, hbm, hbm),
        scratch_shapes=[
            pltpu.VMEM((epochs, tile_rows, tile_cols), bf16),
            pltpu.VMEM((tile_rows, tile_cols), f32),
            pltpu.VMEM((tile_rows, tile_cols), f32),
            pltpu.VMEM((n_grp, share, tile_rows, tile_cols), bf16),
            pltpu.VMEM((others, share, tile_rows, tile_cols), bf16),
            pltpu.VMEM((epochs, ifgs), bf16),
            pltpu.SMEM(rotation.shape, f32),
            pltpu.VMEM((tile_rows, tile_cols), jnp.int32),
            pltpu.VMEM((tile_rows, tile_cols), jnp.int32),
            pltpu.VMEM((epochs * SUB, ifgs * SUB), bf16),
            pltpu.VMEM((n_grp, tile_rows, tile_cols), f32),
            pltpu.VMEM((others, tile_rows, tile_cols), f32),
            pltpu.VMEM((tile_rows + 2 * REACH, tile_cols), f32),
            pltpu.VMEM((tile_rows, tile_cols + 256), f32),
            dma((4 + n_grp,)),
            dma((others, chunks)),
            dma((others, chunks)),
            dma((others,)),
            dma((others,)),
            dma((4,)),
            dma((4,)),
            dma((chunks + 2,)),
            pltpu.VMEM((epochs * SUB, tile_rows // SUB * tile_cols), f32),
        ],
        compiler_params=pltpu.CompilerParams(
            collective_id=0, has_side_effects=True, vmem_limit_bytes=GRANT
        ),
        cost_estimate=pl.CostEstimate(
            flops=2 * epochs * ifgs * SUB * tile_rows * tile_cols,
            bytes_accessed=8 * 1024 * 1024,
            transcendentals=0,
        ),
    )(phase, pseudo_inverse, rotation, plate_id, coherent)
    return pl.pallas_call(
        write_out,
        out_shape=tuple(jax.ShapeDtypeStruct(r.shape, r.dtype) for r in results),
        in_specs=[hbm] * 3,
        out_specs=(hbm,) * 3,
        scratch_shapes=[pltpu.VMEM(r.shape, r.dtype) for r in results]
        + [dma((PIECES + 2,)), dma((PIECES + 2,))],
        compiler_params=pltpu.CompilerParams(vmem_limit_bytes=GRANT),
    )(*results)


def solution(mesh):
    sizes = (mesh.shape["grp"], mesh.shape["row"], mesh.shape["col"])
    return jax.shard_map(
        functools.partial(on_device, sizes),
        mesh=mesh,
        in_specs=(
            P("grp", None, "row", "col"),
            P(),
            P(),
            P(("grp", "row"), "col"),
            P(("grp", "row"), "col"),
        ),
        out_specs=(
            P(None, ("grp", "row"), "col"),
            P(("grp", "row"), "col"),
            P(("grp", "row"), "col"),
        ),
        check_vma=False,
    )
```
